128 devices in a mesh: gen: 8 (over y, core), voc: 16 (over x, z).
Axes of the slice: x: 4, y: 4, z: 4, core: 2. Of those that a mesh axis runs over, the one named last changes fastest.
Arguments:
- features: bfloat16 [8192, 24, 128], P(('gen', 'voc')), may hold values from -6 to 6
- target: int32 [8192], P(('gen', 'voc')), may hold values from -1 to 511, as said below
- extents: int32 [8192, 3], P(('gen', 'voc')), may hold values from 0 to 24, as said below
- w_pre: bfloat16 [896, 1536], replicated, may hold values from -0.1875 to 0.1875
- biases: float32 [1536], replicated, may hold values from -1.5 to 1.5
- snake_params: float32 [2, 1536], replicated, may hold values from 0.4 to 2.5
- w_up: bfloat16 [1536, 6144], replicated, may hold values from -0.109375 to 0.109375
- up_bias: float32 [768], replicated, may hold values from -1.5 to 1.5
Outputs:
- waves: bfloat16 [8192, 96, 768], P(('gen', 'voc'))
The draws below stay inside these ranges and needn't reach their ends.
Inputs may be any that keep to these rules, and one draw needn't show every extreme that they name: Within each gen group every (voc index, slot) pair target[i] = voc index * 32 + slot is named by exactly one generator slot; -1 marks an empty generator slot. No generator device names one vocoder device more than 4 times, and in every group some device does so exactly 4 times for each vocoder device. `extents`: column 0 is 24 except for the last segment of an utterance; columns 1 and 2 are 0 where the stream neighbour belongs to another utterance and equal its column 0 otherwise; all zero for empty slots.
All inputs are finite; a program needn't handle non-finite values.
Results may differ from the reference program's by a relative error of at most 0.0048.
Values may be sent and summed in bfloat16 or wider, within the bound.
No kernel may reach another device: no remote copies, remote signals or barrier semaphores. Data moves between devices by JAX's collectives and lax.ppermute only.
A program may use at most 192 MiB of HBM per device.

```python
import math
import jax
import jax.numpy as jnp
from jax import lax

FEAT = 128
CH = 1536
CH2 = 768
UP = 4
KPRE = 7
SEG = 24
SLOT = 32
RIM = 4
SRC_CAP = 64
CAP = 4
SOURCE_SLOTS = 8192
N_GEN = 8
N_VOC = 16


def stream_plan(key):
    device_count = N_GEN * N_VOC
    stream_len = SLOT * device_count
    key_start, key_last, key_extra, key_sign, key_force = jax.random.split(key, 5)
    cells = jnp.arange(stream_len, dtype=jnp.int32)
    starts = jax.random.randint(key_start, (stream_len,), 0, 5) == 0
    starts = starts | (cells == 0) | (cells == stream_len // 2)
    is_last = jnp.roll(starts, -1)
    last_len = jax.random.randint(key_last, (stream_len,), 1, SEG + 1)
    seg_frames = jnp.where(is_last, last_len, SEG).astype(jnp.int32)
    prev_frames = jnp.where(starts, 0, jnp.roll(seg_frames, 1)).astype(jnp.int32)
    next_frames = jnp.where(is_last, 0, jnp.roll(seg_frames, -1)).astype(jnp.int32)
    half_cap = CAP // 2
    pair_count = N_VOC // 2
    extra = jax.random.randint(key_extra, (N_GEN, N_VOC, pair_count), 0, half_cap + 1)
    forced = jax.random.randint(key_force, (N_GEN, N_VOC), 0, pair_count)
    extra = jnp.where(jnp.arange(pair_count)[None, None, :] == forced[:, :, None], half_cap, extra)
    signs = jax.random.randint(key_sign, (N_GEN, N_VOC, pair_count), 0, 2) * 2 - 1
    counts = jnp.stack([half_cap + signs * extra, half_cap - signs * extra], axis=-1)
    counts = jnp.transpose(counts.reshape(N_GEN, N_VOC, N_VOC), (0, 2, 1)).astype(jnp.int32)
    row_start = jnp.cumsum(counts, axis=2) - counts
    col_start = jnp.cumsum(counts, axis=1) - counts
    slot_ids = jnp.arange(SRC_CAP, dtype=jnp.int32)[None, None, None, :]
    inside = (slot_ids >= row_start[..., None]) & (slot_ids < row_start[..., None] + counts[..., None])
    stream_slot = col_start[..., None] + slot_ids - row_start[..., None]
    worker_ids = jnp.arange(N_VOC, dtype=jnp.int32)[None, None, :, None]
    group_ids = jnp.arange(N_GEN, dtype=jnp.int32)[:, None, None, None]
    codes = worker_ids * SLOT + stream_slot
    places = stream_slot * device_count + group_ids * N_VOC + worker_ids
    used = jnp.any(inside, axis=2)
    target = jnp.where(used, jnp.sum(jnp.where(inside, codes, 0), axis=2), -1)
    position = jnp.where(used, jnp.sum(jnp.where(inside, places, 0), axis=2), 0)
    table = jnp.stack([seg_frames, prev_frames, next_frames], axis=1)
    extents = jnp.where(used[..., None], table[position], 0)
    return (target.reshape(-1).astype(jnp.int32), extents.reshape(-1, 3).astype(jnp.int32))


def draw_target(key, part):
    return stream_plan(key)[0]


def draw_extents(key, part):
    return stream_plan(key)[1]


def level_of(own_key, dims, cuts, smallest, largest):
    level, own = 1.0, jax.random.fold_in(own_key, 6)
    for axis_at, parts in cuts:
        heights = jnp.exp(jax.random.uniform(jax.random.fold_in(own, axis_at), (parts,), jnp.float32, smallest / len(cuts), largest / len(cuts)))
        level = level * jnp.repeat(heights, dims[axis_at] // parts).reshape([-1 if axis == axis_at else 1 for axis in range(len(dims))])
    return level


def gaussian(own_key, extent, deviation, bound, cuts=(), kind=jnp.bfloat16):
    values = deviation * jax.random.normal(own_key, extent, jnp.float32)
    if cuts:
        values = values * level_of(own_key, extent, cuts, -0.22, 0.18)
    return jnp.clip(values, -bound, bound).astype(kind)


def setup_inputs(seed: int = 0) -> dict:
    seeds = jax.random.split(jax.random.key(seed), 9)
    features = gaussian(seeds[0], (SOURCE_SLOTS, SEG, FEAT), 1.0, 6.0, ((0, 128),))
    target = draw_target(jax.random.fold_in(seeds[8], 71), 0)
    extents = draw_extents(jax.random.fold_in(seeds[8], 71), 0)
    w_pre = gaussian(seeds[3], (KPRE * FEAT, CH), (KPRE * FEAT) ** -0.5, 0.1875)
    biases = gaussian(seeds[4], (CH,), 0.3, 1.5, (), jnp.float32)
    snake_params = jnp.clip(jnp.exp(jax.random.uniform(seeds[5], (2, CH), jnp.float32, math.log(0.4), math.log(2.5))), 0.4, 2.5)
    w_up = gaussian(seeds[6], (CH, 2 * UP * CH2), (2 * CH) ** -0.5, 0.109375)
    up_bias = gaussian(seeds[7], (CH2,), 0.3, 1.5, (), jnp.float32)
    return dict(features=features, target=target, extents=extents, w_pre=w_pre, biases=biases, snake_params=snake_params, w_up=w_up, up_bias=up_bias)


def stacked_taps(values, kernel):
    length = values.shape[1] - (kernel - 1)
    pieces = [values[:, tap_index: tap_index + length] for tap_index in range(kernel)]
    return jnp.concatenate(pieces, axis=2)


def convolve(values, weight, kernel):
    stacked = stacked_taps(values, kernel)
    flattened = stacked.reshape(-1, stacked.shape[2])
    result = jnp.dot(flattened, weight, preferred_element_type=jnp.float32)
    return result.reshape(stacked.shape[0], stacked.shape[1], weight.shape[1])


def snake_act(values, alpha, beta):
    return values + jnp.square(jnp.sin(alpha * values)) / beta


def window_mask(extent_rows, seg_len):
    rim_cells = jnp.arange(RIM, dtype=jnp.int32)
    cells = jnp.arange(seg_len, dtype=jnp.int32)
    before = rim_cells[None, :] + seg_len - RIM < extent_rows[:, 1:2]
    own_part = cells[None, :] < extent_rows[:, 0:1]
    after = rim_cells[None, :] < extent_rows[:, 2:3]
    return jnp.concatenate([before, own_part, after], axis=1).astype(jnp.float32)


def trunk(window, frame_mask, w_pre, biases, snake_params):
    first = (KPRE - 1) // 2
    span = window.shape[1]
    inputs = window * frame_mask[:, :, None].astype(jnp.bfloat16)
    hidden = frame_mask[:, first:span - first, None] * (convolve(inputs, w_pre, KPRE) + biases)
    return snake_act(hidden, snake_params[0], snake_params[1]).astype(jnp.bfloat16)


def upsample(activations, seg_mask, w_up, up_bias):
    projected = jnp.dot(activations.reshape(-1, activations.shape[2]), w_up, preferred_element_type=jnp.float32)
    projected = projected.reshape(activations.shape[0], activations.shape[1], 2 * UP, up_bias.shape[0])
    centre = projected[:, 1:-1, UP // 2: UP // 2 + UP]
    side = jnp.concatenate([projected[:, :-2, 3 * UP // 2:], projected[:, 2:, :UP // 2]], axis=2)
    samples = seg_mask[:, :, None, None] * (centre + side + up_bias)
    return samples.astype(jnp.bfloat16).reshape(activations.shape[0], -1, up_bias.shape[0])


def reference(features, target, extents, w_pre, biases, snake_params, w_up, up_bias):
    device_count = N_GEN * N_VOC
    stream_len = SLOT * device_count
    source_ids = jnp.arange(SOURCE_SLOTS, dtype=jnp.int32)
    group_index = source_ids // (SRC_CAP * N_VOC)
    worker = group_index * N_VOC + target // SLOT
    position = jnp.where(target >= 0, (target % SLOT) * device_count + worker, stream_len).astype(jnp.int32)
    stream_feat = jnp.zeros((stream_len, SEG, FEAT), jnp.bfloat16).at[position].set(features, mode="drop")
    stream_ext = jnp.zeros((stream_len, 3), jnp.int32).at[position].set(extents, mode="drop")
    windows = jnp.concatenate([jnp.roll(stream_feat, 1, axis=0)[:, SEG - RIM:], stream_feat,
                               jnp.roll(stream_feat, -1, axis=0)[:, :RIM]], axis=1)
    window_masks = window_mask(stream_ext, SEG)

    def vocode(block_pair):
        window_block, mask_block = block_pair
        activations = trunk(window_block, mask_block, w_pre, biases, snake_params)
        return upsample(activations, mask_block[:, RIM:RIM + SEG], w_up, up_bias)

    outputs = lax.map(vocode, (windows.reshape(device_count, SLOT, SEG + 2 * RIM, FEAT),
                               window_masks.reshape(device_count, SLOT, SEG + 2 * RIM)))
    outputs = outputs.reshape(stream_len, SEG * UP, CH2)
    gathered = outputs[jnp.clip(position, 0, stream_len - 1)]
    return jnp.where((target >= 0)[:, None, None], gathered, jnp.zeros_like(gathered))
```

```python
import functools

import jax
import jax.numpy as jnp
from jax import lax
from jax.experimental import pallas as pl
from jax.experimental.pallas import tpu as pltpu
from jax.sharding import PartitionSpec as P

UP = 4
KPRE = 7
RIM = 4
CAP = 4
LANES = 128

SIN2 = (9.869604311707747, -32.46967117172015, 42.72719633651888, -30.101465841328583, 13.050098920339147, -3.3565926218240247)


def copy_of(src, dst, sem):
    return pltpu.make_async_copy(src, dst, sem)


def vocode_kernel(starts, frames, block, rims, target, extents, features, *rest):
    if rims:
        home, w_pre, biases, snake, w_up, up_bias, _, out = rest[:8]
        scratch = rest[8:]
    else:
        home = None
        w_pre, biases, snake, w_up, up_bias, out = rest[:6]
        scratch = rest[6:]
    (wp, wu, win, msk, taps, acts, rows32, stage, zeros, slots, ranks, counts, w_sem, out_sem, zero_sem) = scratch
    pieces = len(starts)
    act_rows = frames + 2
    win_rows = frames + 8
    seg = features.shape[1]
    channels = wp.shape[1]
    width = up_bias.shape[1]
    n_slots = target.shape[0]
    span = UP * frames

    copy_of(w_pre, wp, w_sem.at[8]).start()
    order = (2, 6, 3, 7, 4, 0, 5, 1)
    for tap in order:
        cols = pl.ds(tap * width, width)
        copy_of(w_up.at[:, cols], wu.at[:, cols], w_sem.at[tap]).start()

    if not rims:
        zeros[...] = jnp.zeros_like(zeros)
    for v in range(16):
        counts[v] = 0
    slots[0] = 0
    ranks[0] = 0

    def scan(i, found):
        code = target[i]
        used = code >= 0

        @pl.when(used)
        def _():
            worker = code // 32
            rank = counts[worker]
            slots[found] = i
            ranks[found] = rank
            counts[worker] = rank + 1

        if not rims:

            @pl.when(jnp.logical_not(used))
            def _():
                copy_of(zeros, out.at[i], zero_sem.at[i]).start()

        return found + used.astype(jnp.int32)

    found = lax.fori_loop(0, n_slots, scan, jnp.int32(0))
    n_blocks = (found + block - 1) // block

    cell = lax.broadcasted_iota(jnp.int32, (seg, LANES), 0)
    rim_cell = lax.broadcasted_iota(jnp.int32, (2 * RIM, LANES), 0)

    def fill(first, b):
        c = jnp.minimum(first + b, found - 1)
        slot = slots[c]
        own = (cell < extents[slot, 0]).astype(jnp.float32)
        values = features[slot].astype(jnp.float32) * own
        if not rims:
            win[0, pl.ds(b, seg, stride=block), :] = values
            msk[0, pl.ds(b, seg, stride=block), :] = own
        else:
            at = RIM * block + b
            inner = win_rows - RIM
            win[0, pl.ds(at, inner, stride=block), :] = values[:inner]
            msk[0, pl.ds(at, inner, stride=block), :] = own[:inner]
            win[1, pl.ds(b, inner, stride=block), :] = values[seg - inner :]
            msk[1, pl.ds(b, inner, stride=block), :] = own[seg - inner :]
            worker = target[slot] // 32
            rank = ranks[c]
            before_ok = (rim_cell - RIM + seg - RIM < extents[slot, 1]).astype(jnp.float32)
            after_ok = (rim_cell < extents[slot, 2]).astype(jnp.float32)
            before = home[worker, rank].astype(jnp.float32) * before_ok
            after = home[lax.rem(worker + 1, 16), rank].astype(jnp.float32) * after_ok
            win[0, pl.ds(b, RIM, stride=block), :] = before[RIM:]
            msk[0, pl.ds(b, RIM, stride=block), :] = before_ok[RIM:]
            tail = inner * block + b
            win[1, pl.ds(tail, RIM, stride=block), :] = after[:RIM]
            msk[1, pl.ds(tail, RIM, stride=block), :] = after_ok[:RIM]

    def drain(blk):
        buf = lax.rem(blk, 2)

        def one(b, carry):
            @pl.when(blk * block + b < found)
            def _():
                for p in range(pieces):
                    copy_of(stage.at[buf, p, b], out.at[0, pl.ds(0, span)], out_sem.at[buf, p, b]).wait()

            return carry

        lax.fori_loop(0, block, one, 0)

    def body(blk, carry):
        first = blk * block
        buf = lax.rem(blk, 2)

        def fill_one(b, c):
            fill(first, b)
            return c

        lax.fori_loop(0, block, fill_one, 0)

        for p in range(pieces):
            for q in range(KPRE):
                taps[pl.ds(p * act_rows * block, act_rows * block), pl.ds(q * LANES, LANES)] = win[
                    p, pl.ds(q * block, act_rows * block), :
                ].astype(jnp.bfloat16)

        @pl.when(blk == 0)
        def _():
            copy_of(w_pre, wp, w_sem.at[8]).wait()

        step = 256

        def conv_chunk(n, c):
            cols = pl.ds(pl.multiple_of(n * step, step), step)
            bias = biases[:, cols]
            scale = snake[0:1, cols] * (1.0 / jnp.pi)
            inverse = 1.0 / snake[1:2, cols]
            for p in range(pieces):
                sums = jnp.dot(
                    taps[pl.ds(p * act_rows * block, act_rows * block), :],
                    wp[:, cols],
                    preferred_element_type=jnp.float32,
                )
                mask = msk[p, pl.ds(3 * block, act_rows * block), :]
                hidden = jnp.concatenate([mask, mask], axis=1) * (sums + bias)
                turns = hidden * scale
                rest_of = turns - jnp.floor(turns + 0.5)
                u = rest_of * rest_of
                poly = SIN2[-1] * u + SIN2[-2]
                for coef in SIN2[-3::-1]:
                    poly = poly * u + coef
                acts[p, :, cols] = (hidden + u * poly * inverse).astype(jnp.bfloat16)
            return c

        lax.fori_loop(0, channels // step, conv_chunk, 0)

        @pl.when(blk >= 2)
        def _():
            drain(blk - 2)

        for r in range(UP):
            centre_tap = r + UP // 2
            side_tap = r + UP + UP // 2 if r < UP // 2 else r - UP // 2
            side_at = 0 if r < UP // 2 else 2 * block

            @pl.when(blk == 0)
            def _():
                for tap in (centre_tap, side_tap):
                    cols = pl.ds(tap * width, width)
                    copy_of(w_up.at[:, cols], wu.at[:, cols], w_sem.at[tap]).wait()

            def up_chunk(n, c):
                at = pl.multiple_of(n * step, step)
                centre = acts[:, pl.ds(block, frames * block), :].reshape(-1, channels)
                side = acts[:, pl.ds(side_at, frames * block), :].reshape(-1, channels)
                sums = jnp.dot(
                    centre, wu[:, pl.ds(centre_tap * width + at, step)], preferred_element_type=jnp.float32
                ) + jnp.dot(side, wu[:, pl.ds(side_tap * width + at, step)], preferred_element_type=jnp.float32)
                sums = sums + up_bias[:, pl.ds(at, step)]
                for p in range(pieces):
                    for j in range(frames):
                        mask = msk[p, pl.ds((j + 4) * block, block), :]
                        here = (p * frames + j) * block
                        for half in range(step // LANES):
                            rows32[
                                n * (step // LANES) + half,
                                pl.ds(p * block * span + UP * j + r, block, stride=span),
                                :,
                            ] = mask * sums[here : here + block, half * LANES : (half + 1) * LANES]
                return c

            lax.fori_loop(0, width // step, up_chunk, 0)

        def send(b, c):
            for p in range(pieces):
                for n in range(width // LANES):
                    stage[buf, p, b, :, n * LANES : (n + 1) * LANES] = rows32[
                        n, pl.ds((p * block + b) * span, span), :
                    ].astype(jnp.bfloat16)

            @pl.when(first + b < found)
            def _():
                slot = slots[first + b]
                for p in range(pieces):
                    copy_of(
                        stage.at[buf, p, b], out.at[slot, pl.ds(UP * starts[p], span)], out_sem.at[buf, p, b]
                    ).start()

            return c

        lax.fori_loop(0, block, send, 0)
        return carry

    lax.fori_loop(0, n_blocks, body, 0)

    @pl.when(n_blocks == 0)
    def _():
        copy_of(w_pre, wp, w_sem.at[8]).wait()
        for tap in range(2 * UP):
            cols = pl.ds(tap * width, width)
            copy_of(w_up.at[:, cols], wu.at[:, cols], w_sem.at[tap]).wait()

    @pl.when(n_blocks >= 2)
    def _():
        drain(n_blocks - 2)

    @pl.when(n_blocks >= 1)
    def _():
        drain(n_blocks - 1)

    if not rims:

        def settle(i, c):
            @pl.when(target[i] < 0)
            def _():
                copy_of(zeros, out.at[i], zero_sem.at[i]).wait()

            return c

        lax.fori_loop(0, n_slots, settle, 0)


def vocode(starts, frames, block, home, waves, target, extents, features, w_pre, biases, snake, w_up, up_bias):
    rims = home is not None
    pieces = len(starts)
    n_slots, seg, feat = features.shape
    channels = w_pre.shape[1]
    width = up_bias.shape[1]
    span = UP * frames
    smem = pl.BlockSpec(memory_space=pltpu.SMEM)
    vmem = pl.BlockSpec(memory_space=pltpu.VMEM)
    hbm = pl.BlockSpec(memory_space=pl.ANY)
    operands = [target, extents, features]
    specs = [smem, smem, vmem]
    if rims:
        operands.append(home)
        specs.append(vmem)
    operands += [w_pre, biases, snake, w_up, up_bias]
    specs += [hbm, vmem, vmem, hbm, vmem]
    aliases = {}
    if rims:
        aliases = {len(operands): 0}
        operands.append(waves)
        specs.append(hbm)
    return pl.pallas_call(
        functools.partial(vocode_kernel, starts, frames, block, rims),
        out_shape=jax.ShapeDtypeStruct((n_slots, UP * seg, width), jnp.bfloat16),
        in_specs=specs,
        out_specs=hbm,
        input_output_aliases=aliases,
        scratch_shapes=[
            pltpu.VMEM(w_pre.shape, jnp.bfloat16),
            pltpu.VMEM(w_up.shape, jnp.bfloat16),
            pltpu.VMEM((pieces, (frames + 8) * block, feat), jnp.float32),
            pltpu.VMEM((pieces, (frames + 8) * block, feat), jnp.float32),
            pltpu.VMEM((pieces * (frames + 2) * block, KPRE * feat), jnp.bfloat16),
            pltpu.VMEM((pieces, (frames + 2) * block, channels), jnp.bfloat16),
            pltpu.VMEM((width // LANES, pieces * block * span, LANES), jnp.float32),
            pltpu.VMEM((2, pieces, block, span, width), jnp.bfloat16),
            pltpu.VMEM((16, LANES) if rims else (UP * seg, width), jnp.bfloat16),
            pltpu.SMEM((n_slots,), jnp.int32),
            pltpu.SMEM((n_slots,), jnp.int32),
            pltpu.SMEM((16,), jnp.int32),
            pltpu.SemaphoreType.DMA((9,)),
            pltpu.SemaphoreType.DMA((2, pieces, block)),
            pltpu.SemaphoreType.DMA((n_slots,)),
        ],
        compiler_params=pltpu.CompilerParams(vmem_limit_bytes=58 * 2**20),
        cost_estimate=pl.CostEstimate(
            flops=2 * 48 * pieces * frames * 2 * channels * UP * width,
            bytes_accessed=2 * (w_up.size + w_pre.size + 48 * pieces * span * width),
            transcendentals=0,
        ),
        name="edges" if rims else "inner",
    )(*operands)


def one_hot_rows(match, values):
    rows = jnp.dot(match.astype(jnp.bfloat16), values.reshape(values.shape[0], -1), preferred_element_type=jnp.float32)
    return rows.astype(jnp.bfloat16)


def packed(features, target):
    n_slots, seg, feat = features.shape
    used = target >= 0
    worker = jnp.where(used, target // 32, -1)
    hot = (worker[:, None] == jnp.arange(16, dtype=jnp.int32)[None, :]).astype(jnp.int32)
    rank = jnp.sum((jnp.cumsum(hot, axis=0) - hot) * hot, axis=1)
    row = jnp.where(used, worker * CAP + rank, -1)
    select = row[None, :] == jnp.arange(16 * CAP, dtype=jnp.int32)[:, None]
    code = jnp.sum(jnp.where(select, (target % 32 + 1)[None, :], 0), axis=1).astype(jnp.bfloat16)
    heads = one_hot_rows(select, features[:, :RIM]).reshape(16, CAP, RIM, feat)
    tails = one_hot_rows(select, features[:, seg - RIM :]).reshape(16, CAP, RIM, feat)
    tails = jnp.roll(tails, 1, axis=0)
    code = code.reshape(16, CAP)
    codes = jnp.concatenate([jnp.roll(code, 1, axis=0), code], axis=1)
    codes = jnp.broadcast_to(codes[:, None, :, None], (16, 1, 2 * CAP, feat))
    return jnp.concatenate([jnp.concatenate([tails, heads], axis=2), codes], axis=1)


def swapped(got, lower, upper):
    gen, voc = lax.axis_index("gen"), lax.axis_index("voc")
    last = lax.axis_size("gen") - 1
    wraps = voc == 0
    lower = jnp.where(wraps, lower, got)
    upper = jnp.where(wraps, upper, got)

    def codes(block, first):
        return block[:, CAP, first : first + CAP, 0].astype(jnp.int32).reshape(-1)

    def entries(block, first):
        return block[:, :CAP, first : first + RIM]

    tail_code, head_code = codes(got, 0), codes(got, RIM)
    far_tail, far_head = codes(lower, 0), codes(upper, RIM)
    far_tail = jnp.where(wraps & (gen == 0) & (far_tail > 0), far_tail % 32 + 1, far_tail)
    far_head = jnp.where(wraps & (gen == last) & (far_head > 0), (far_head + 30) % 32 + 1, far_head)
    next_match = (tail_code[:, None] == far_head[None, :]) & (tail_code[:, None] > 0)
    prev_match = (head_code[:, None] == far_tail[None, :]) & (head_code[:, None] > 0)
    shape = (got.shape[0], CAP, RIM, got.shape[3])
    heads = one_hot_rows(next_match, entries(upper, RIM).reshape(64, -1)).reshape(shape)
    tails = one_hot_rows(prev_match, entries(lower, 0).reshape(64, -1)).reshape(shape)
    return jnp.concatenate([heads, tails], axis=2)


def on_device(features, target, extents, w_pre, biases, snake_params, w_up, up_bias):
    n_gen, n_voc = lax.axis_size("gen"), lax.axis_size("voc")
    got = lax.all_to_all(packed(features, target), "voc", split_axis=0, concat_axis=0, tiled=True)
    lower = lax.ppermute(got, ("gen", "voc"), [(g * n_voc, (g + 1) % n_gen * n_voc) for g in range(n_gen)])
    upper = lax.ppermute(got, ("gen", "voc"), [(g * n_voc, (g - 1) % n_gen * n_voc) for g in range(n_gen)])
    home = lax.all_to_all(swapped(got, lower, upper), "voc", split_axis=0, concat_axis=0, tiled=True)
    rest = (target, extents, features, w_pre, biases[None, :], snake_params, w_up, up_bias[None, :])
    waves = vocode((RIM,), 16, 16, None, None, *rest)
    return vocode((0, 20), 4, 32, home, waves, *rest)


def solution(mesh):
    split = P(("gen", "voc"))
    return jax.shard_map(
        on_device,
        mesh=mesh,
        in_specs=(split, split, split, P(), P(), P(), P(), P()),
        out_specs=split,
        check_vma=False,
    )
```

```python
import functools

import jax
import jax.numpy as jnp
from jax import lax
from jax.experimental import pallas as pl
from jax.experimental.pallas import tpu as pltpu
from jax.sharding import PartitionSpec as P

UP = 4
KPRE = 7
RIM = 4
CAP = 4
LANES = 128
STEP = 256

SIN2 = (9.869604311707747, -32.46967117172015, 42.72719633651888, -30.101465841328583, 13.050098920339147, -3.3565926218240247)


def copy_of(src, dst, sem):
    return pltpu.make_async_copy(src, dst, sem)


def vocode_kernel(starts, frames, rims, target, extents, features, *rest):
    if rims:
        home, w_pre, biases, snake, w_up, up_bias, _, out = rest[:8]
        scratch = rest[8:]
    else:
        home = None
        w_pre, biases, snake, w_up, up_bias, out = rest[:6]
        scratch = rest[6:]
    (wp, wu, win, msk, taps, acts, rows32, stage, zeros, slots, ranks, counts, w_sem, out_sem, zero_sem) = scratch
    pieces = len(starts)
    act_rows = frames + 2
    win_rows = frames + 8
    seg = features.shape[1]
    channels = wp.shape[1]
    width = up_bias.shape[1]
    n_slots = target.shape[0]
    span = UP * frames
    pitch = span + 8
    parts = width // STEP
    tiles = STEP // LANES

    phases = tuple((r + UP // 2, r + UP + UP // 2 if r < UP // 2 else r - UP // 2) for r in range(UP))

    def load_taps(n, start):
        for tap in sum(phases, ()):
            cols = pl.ds(pl.multiple_of(tap * width + n * STEP, STEP), STEP)
            copy = copy_of(w_up.at[:, cols], wu.at[:, cols], w_sem.at[n, tap])
            copy.start() if start else copy.wait()

    def load_pre(start):
        copy = copy_of(w_pre, wp, w_sem.at[parts, 0])
        copy.start() if start else copy.wait()

    load_pre(True)
    for v in range(17):
        counts[v] = 0
    slots[0] = 0
    ranks[0] = 0

    def scan(i, found):
        code = target[i]
        used = code >= 0
        slots[found] = i
        if rims:
            worker = jnp.where(used, lax.shift_right_logical(code, 5), 16)
            rank = counts[worker]
            ranks[found] = rank
            counts[worker] = rank + 1
        return found + used.astype(jnp.int32)

    found = lax.fori_loop(0, n_slots, scan, jnp.int32(0), unroll=8)

    cell = lax.broadcasted_iota(jnp.int32, (seg, LANES), 0)
    rim_cell = lax.broadcasted_iota(jnp.int32, (2 * RIM, LANES), 0)

    def fill(block, b):
        c = jnp.minimum(b, found - 1)
        slot = slots[c]
        own = (cell < extents[slot, 0]).astype(jnp.float32)
        values = features[slot].astype(jnp.float32) * own
        if not rims:
            win[0, pl.ds(b, seg, stride=block), :] = values
            msk[0, pl.ds(b, seg, stride=block), :] = own
        else:
            at = RIM * block + b
            inner = win_rows - RIM
            win[0, pl.ds(at, inner, stride=block), :] = values[:inner]
            msk[0, pl.ds(at, inner, stride=block), :] = own[:inner]
            win[1, pl.ds(b, inner, stride=block), :] = values[seg - inner :]
            msk[1, pl.ds(b, inner, stride=block), :] = own[seg - inner :]
            worker = lax.shift_right_logical(target[slot], 5)
            rank = ranks[c]
            before_ok = (rim_cell - RIM + seg - RIM < extents[slot, 1]).astype(jnp.float32)
            after_ok = (rim_cell < extents[slot, 2]).astype(jnp.float32)
            before = home[worker, rank].astype(jnp.float32) * before_ok
            after = home[(worker + 1) & 15, rank].astype(jnp.float32) * after_ok
            win[0, pl.ds(b, RIM, stride=block), :] = before[RIM:]
            msk[0, pl.ds(b, RIM, stride=block), :] = before_ok[RIM:]
            tail = inner * block + b
            win[1, pl.ds(tail, RIM, stride=block), :] = after[:RIM]
            msk[1, pl.ds(tail, RIM, stride=block), :] = after_ok[:RIM]

    def run(block):
        rows = act_rows * block

        def fill_one(b, c):
            fill(block, b)
            return c

        lax.fori_loop(0, block, fill_one, 0, unroll=2)
        for p in range(pieces):
            for q in range(KPRE):
                taps[pl.ds(p * rows, rows), pl.ds(q * LANES, LANES)] = win[p, pl.ds(q * block, rows), :].astype(
                    jnp.bfloat16
                )

        load_pre(False)
        for n in range(parts):
            load_taps(n, True)

        if not rims:
            zeros[...] = jnp.zeros_like(zeros)

            def clear(i, c):
                @pl.when(target[i] < 0)
                def _():
                    copy_of(zeros, out.at[i], zero_sem.at[i]).start()

                return c

            lax.fori_loop(0, n_slots, clear, 0)

        def conv_chunk(n, c):
            cols = pl.ds(pl.multiple_of(n * STEP, STEP), STEP)
            bias = biases[:, cols]
            scale = snake[0:1, cols] * (1.0 / jnp.pi)
            inverse = 1.0 / snake[1:2, cols]
            for p in range(pieces):
                sums = jnp.dot(taps[pl.ds(p * rows, rows), :], wp[:, cols], preferred_element_type=jnp.float32)
                mask = msk[p, pl.ds(3 * block, rows), :]
                hidden = jnp.concatenate([mask] * tiles, axis=1) * (sums + bias)
                turns = hidden * scale
                rest_of = turns - jnp.floor(turns + 0.5)
                u = rest_of * rest_of
                poly = SIN2[-1] * u + SIN2[-2]
                for coef in SIN2[-3::-1]:
                    poly = poly * u + coef
                acts[pl.ds(p * rows, rows), cols] = (hidden + u * poly * inverse).astype(jnp.bfloat16)
            return c

        lax.fori_loop(0, channels // STEP, conv_chunk, 0, unroll=2)

        def acts_from(shift):
            picked = [acts[pl.ds(p * rows + shift * block, frames * block), :] for p in range(pieces)]
            return picked[0] if pieces == 1 else jnp.concatenate(picked, axis=0)

        def up_part(n, c):
            load_taps(n, False)
            for r in range(UP):
                sums = up_bias[:, pl.ds(pl.multiple_of(n * STEP, STEP), STEP)]
                for tap, shift in zip(phases[r], (1, 0 if r < UP // 2 else 2)):
                    cols = pl.ds(pl.multiple_of(tap * width + n * STEP, STEP), STEP)
                    sums = sums + jnp.dot(acts_from(shift), wu[:, cols], preferred_element_type=jnp.float32)
                for p in range(pieces):
                    for j in range(frames):
                        mask = msk[p, pl.ds((j + 4) * block, block), :]
                        here = (p * frames + j) * block
                        for half in range(tiles):
                            rows32[
                                n * tiles + half, pl.ds(p * block * pitch + UP * j + r, block, stride=pitch), :
                            ] = mask * sums[here : here + block, half * LANES : (half + 1) * LANES]
            return c

        lax.fori_loop(0, parts, up_part, 0)

        def send(b, c):
            for p in range(pieces):
                for n in range(width // LANES):
                    stage[p, b, :, n * LANES : (n + 1) * LANES] = rows32[
                        n, pl.ds(pl.multiple_of((p * block + b) * pitch, 8), span), :
                    ].astype(jnp.bfloat16)

            @pl.when(b < found)
            def _():
                for p in range(pieces):
                    copy_of(stage.at[p, b], out.at[slots[b], pl.ds(UP * starts[p], span)], out_sem.at[p, b]).start()

            return c

        lax.fori_loop(0, block, send, 0)

    for units in range(1, 5):

        @pl.when((found > 16 * (units - 1)) & (found <= 16 * units))
        def _(units=units):
            run(16 * units)

    @pl.when(found == 0)
    def _():
        load_pre(False)
        if not rims:
            zeros[...] = jnp.zeros_like(zeros)

            def clear(i, c):
                copy_of(zeros, out.at[i], zero_sem.at[i]).start()
                return c

            lax.fori_loop(0, n_slots, clear, 0)

    def settle(b, c):
        @pl.when(b < found)
        def _():
            for p in range(pieces):
                copy_of(stage.at[p, b], out.at[0, pl.ds(0, span)], out_sem.at[p, b]).wait()

        if not rims:

            @pl.when(target[b] < 0)
            def _():
                copy_of(zeros, out.at[b], zero_sem.at[b]).wait()

        return c

    lax.fori_loop(0, n_slots, settle, 0)


def vocode(starts, frames, home, waves, target, extents, features, w_pre, biases, snake, w_up, up_bias):
    rims = home is not None
    pieces = len(starts)
    n_slots, seg, feat = features.shape
    channels = w_pre.shape[1]
    width = up_bias.shape[1]
    span = UP * frames
    pitch = span + 8
    smem = pl.BlockSpec(memory_space=pltpu.SMEM)
    vmem = pl.BlockSpec(memory_space=pltpu.VMEM)
    hbm = pl.BlockSpec(memory_space=pl.ANY)
    operands = [target, extents, features]
    specs = [smem, smem, vmem]
    if rims:
        operands.append(home)
        specs.append(vmem)
    operands += [w_pre, biases, snake, w_up, up_bias]
    specs += [hbm, vmem, vmem, hbm, vmem]
    aliases = {}
    if rims:
        aliases = {len(operands): 0}
        operands.append(waves)
        specs.append(hbm)
    return pl.pallas_call(
        functools.partial(vocode_kernel, starts, frames, rims),
        out_shape=jax.ShapeDtypeStruct((n_slots, UP * seg, width), jnp.bfloat16),
        in_specs=specs,
        out_specs=hbm,
        input_output_aliases=aliases,
        scratch_shapes=[
            pltpu.VMEM(w_pre.shape, jnp.bfloat16),
            pltpu.VMEM(w_up.shape, jnp.bfloat16),
            pltpu.VMEM((pieces, (frames + 8) * n_slots, feat), jnp.float32),
            pltpu.VMEM((pieces, (frames + 8) * n_slots, feat), jnp.float32),
            pltpu.VMEM((pieces * (frames + 2) * n_slots, KPRE * feat), jnp.bfloat16),
            pltpu.VMEM((pieces * (frames + 2) * n_slots, channels), jnp.bfloat16),
            pltpu.VMEM((width // LANES, pieces * n_slots * (span + 8), LANES), jnp.float32),
            pltpu.VMEM((pieces, n_slots, span, width), jnp.bfloat16),
            pltpu.VMEM((16, LANES) if rims else (UP * seg, width), jnp.bfloat16),
            pltpu.SMEM((n_slots + 1,), jnp.int32),
            pltpu.SMEM((n_slots + 1,), jnp.int32),
            pltpu.SMEM((17,), jnp.int32),
            pltpu.SemaphoreType.DMA((width // STEP + 1, 2 * UP)),
            pltpu.SemaphoreType.DMA((pieces, n_slots)),
            pltpu.SemaphoreType.DMA((n_slots,)),
        ],
        compiler_params=pltpu.CompilerParams(vmem_limit_bytes=58 * 2**20),
        cost_estimate=pl.CostEstimate(
            flops=2 * 48 * pieces * frames * 2 * channels * UP * width,
            bytes_accessed=2 * (w_up.size + w_pre.size + 48 * pieces * span * width),
            transcendentals=0,
        ),
        name="edges" if rims else "inner",
    )(*operands)


def one_hot_rows(match, values):
    rows = jnp.dot(match.astype(jnp.bfloat16), values.reshape(values.shape[0], -1), preferred_element_type=jnp.float32)
    return rows.astype(jnp.bfloat16)


def packed(features, target):
    n_slots, seg, feat = features.shape
    used = target >= 0
    worker = jnp.where(used, target // 32, -1)
    hot = (worker[:, None] == jnp.arange(16, dtype=jnp.int32)[None, :]).astype(jnp.int32)
    rank = jnp.sum((jnp.cumsum(hot, axis=0) - hot) * hot, axis=1)
    row = jnp.where(used, worker * CAP + rank, -1)
    select = row[None, :] == jnp.arange(16 * CAP, dtype=jnp.int32)[:, None]
    code = jnp.sum(jnp.where(select, (target % 32 + 1)[None, :], 0), axis=1).astype(jnp.bfloat16)
    heads = one_hot_rows(select, features[:, :RIM]).reshape(16, CAP, RIM, feat)
    tails = one_hot_rows(select, features[:, seg - RIM :]).reshape(16, CAP, RIM, feat)
    tails = jnp.roll(tails, 1, axis=0)
    code = code.reshape(16, CAP)
    codes = jnp.concatenate([jnp.roll(code, 1, axis=0), code], axis=1)
    codes = jnp.broadcast_to(codes[:, None, :, None], (16, 1, 2 * CAP, feat))
    return jnp.concatenate([jnp.concatenate([tails, heads], axis=2), codes], axis=1)


def swapped(got, lower, upper):
    gen, voc = lax.axis_index("gen"), lax.axis_index("voc")
    last = lax.axis_size("gen") - 1
    wraps = voc == 0
    lower = jnp.where(wraps, lower, got)
    upper = jnp.where(wraps, upper, got)

    def codes(block, first):
        return block[:, CAP, first : first + CAP, 0].astype(jnp.int32).reshape(-1)

    def entries(block, first):
        return block[:, :CAP, first : first + RIM]

    tail_code, head_code = codes(got, 0), codes(got, RIM)
    far_tail, far_head = codes(lower, 0), codes(upper, RIM)
    far_tail = jnp.where(wraps & (gen == 0) & (far_tail > 0), far_tail % 32 + 1, far_tail)
    far_head = jnp.where(wraps & (gen == last) & (far_head > 0), (far_head + 30) % 32 + 1, far_head)
    next_match = (tail_code[:, None] == far_head[None, :]) & (tail_code[:, None] > 0)
    prev_match = (head_code[:, None] == far_tail[None, :]) & (head_code[:, None] > 0)
    shape = (got.shape[0], CAP, RIM, got.shape[3])
    heads = one_hot_rows(next_match, entries(upper, RIM).reshape(64, -1)).reshape(shape)
    tails = one_hot_rows(prev_match, entries(lower, 0).reshape(64, -1)).reshape(shape)
    return jnp.concatenate([heads, tails], axis=2)


def on_device(features, target, extents, w_pre, biases, snake_params, w_up, up_bias):
    n_gen, n_voc = lax.axis_size("gen"), lax.axis_size("voc")
    got = lax.all_to_all(packed(features, target), "voc", split_axis=0, concat_axis=0, tiled=True)
    lower = lax.ppermute(got, ("gen", "voc"), [(g * n_voc, (g + 1) % n_gen * n_voc) for g in range(n_gen)])
    upper = lax.ppermute(got, ("gen", "voc"), [(g * n_voc, (g - 1) % n_gen * n_voc) for g in range(n_gen)])
    home = lax.all_to_all(swapped(got, lower, upper), "voc", split_axis=0, concat_axis=0, tiled=True)
    rest = (target, extents, features, w_pre, biases[None, :], snake_params, w_up, up_bias[None, :])
    waves = vocode((RIM,), 16, None, None, *rest)
    return vocode((0, 20), 4, home, waves, *rest)


def solution(mesh):
    split = P(("gen", "voc"))
    return jax.shard_map(
        on_device,
        mesh=mesh,
        in_specs=(split, split, split, P(), P(), P(), P(), P()),
        out_specs=split,
        check_vma=False,
    )
```

```python
import functools

import jax
import jax.numpy as jnp
from jax import lax
from jax.experimental import pallas as pl
from jax.experimental.pallas import tpu as pltpu
from jax.sharding import PartitionSpec as P

UP = 4
KPRE = 7
RIM = 4
CAP = 4
LANES = 128
STEP = 256

SIN2 = (9.869604311707747, -32.46967117172015, 42.72719633651888, -30.101465841328583, 13.050098920339147, -3.3565926218240247)


def copy_of(src, dst, sem):
    return pltpu.make_async_copy(src, dst, sem)


def vocode_kernel(starts, frames, rims, plan, features, *rest):
    if rims:
        home, w_pre, w_up, vectors, _, out = rest[:6]
        scratch = rest[6:]
    else:
        home = None
        w_pre, w_up, vectors, out = rest[:4]
        scratch = rest[4:]
    (wp, wu, win, msk, taps, acts, rows32, stage, zeros, slots, ranks, counts, w_sem, out_sem, zero_sem) = scratch
    pieces = len(starts)
    act_rows = frames + 2
    win_rows = frames + 8
    seg = features.shape[1]
    channels = wp.shape[1]
    width = wu.shape[1] // (2 * UP)
    n_slots = features.shape[0]
    span = UP * frames
    pitch = span + 8
    parts = width // STEP
    tiles = STEP // LANES

    phases = tuple((r + UP // 2, r + UP + UP // 2 if r < UP // 2 else r - UP // 2) for r in range(UP))

    def load_taps(n, start):
        for tap in sum(phases, ()):
            cols = pl.ds(pl.multiple_of(tap * width + n * STEP, STEP), STEP)
            copy = copy_of(w_up.at[:, cols], wu.at[:, cols], w_sem.at[n, tap])
            copy.start() if start else copy.wait()

    def load_pre(start):
        copy = copy_of(w_pre, wp, w_sem.at[parts, 0])
        copy.start() if start else copy.wait()

    load_pre(True)
    for n in range(parts):
        load_taps(n, True)
    for v in range(17):
        counts[v] = 0
    slots[0] = 0
    ranks[0] = 0

    def scan(i, found):
        code = plan[i]
        used = code >= 0
        slots[found] = i
        if rims:
            worker = jnp.where(used, lax.shift_right_logical(code, 5), 16)
            rank = counts[worker]
            ranks[found] = rank
            counts[worker] = rank + 1
        return found + used.astype(jnp.int32)

    found = lax.fori_loop(0, n_slots, scan, jnp.int32(0), unroll=8)

    cell = lax.broadcasted_iota(jnp.int32, (seg, LANES), 0)
    rim_cell = lax.broadcasted_iota(jnp.int32, (2 * RIM, LANES), 0)

    def fill(block, b):
        c = jnp.minimum(b, found - 1)
        slot = slots[c]
        own = (cell < plan[n_slots + slot * 3]).astype(jnp.float32)
        values = features[slot].astype(jnp.float32) * own
        if not rims:
            win[0, pl.ds(b, seg, stride=block), :] = values
            msk[0, pl.ds(b, seg, stride=block), :] = own
        else:
            at = RIM * block + b
            inner = win_rows - RIM
            win[0, pl.ds(at, inner, stride=block), :] = values[:inner]
            msk[0, pl.ds(at, inner, stride=block), :] = own[:inner]
            win[1, pl.ds(b, inner, stride=block), :] = values[seg - inner :]
            msk[1, pl.ds(b, inner, stride=block), :] = own[seg - inner :]
            worker = lax.shift_right_logical(plan[slot], 5)
            rank = ranks[c]
            before_ok = (rim_cell - RIM + seg - RIM < plan[n_slots + slot * 3 + 1]).astype(jnp.float32)
            after_ok = (rim_cell < plan[n_slots + slot * 3 + 2]).astype(jnp.float32)
            before = home[worker, rank].astype(jnp.float32) * before_ok
            after = home[(worker + 1) & 15, rank].astype(jnp.float32) * after_ok
            win[0, pl.ds(b, RIM, stride=block), :] = before[RIM:]
            msk[0, pl.ds(b, RIM, stride=block), :] = before_ok[RIM:]
            tail = inner * block + b
            win[1, pl.ds(tail, RIM, stride=block), :] = after[:RIM]
            msk[1, pl.ds(tail, RIM, stride=block), :] = after_ok[:RIM]

            def far(row, rows_from):
                code = (plan[slot] & 31).astype(jnp.float32) + 1.0

                def look(k, total):
                    codes = home[k, 2 * CAP].astype(jnp.float32)
                    for e in range(CAP):
                        entry = home[k, CAP + e].astype(jnp.float32)
                        total = total + jnp.where(codes[row + e : row + e + 1] == code, entry, 0.0)
                    return total

                total = lax.fori_loop(0, home.shape[0], look, jnp.zeros((2 * RIM, LANES), jnp.float32), unroll=8)
                return total[rows_from : rows_from + RIM]

            @pl.when(worker == 0)
            def _():
                win[0, pl.ds(b, RIM, stride=block), :] = far(0, 0) * before_ok[RIM:]

            @pl.when(worker == 15)
            def _():
                win[1, pl.ds(tail, RIM, stride=block), :] = far(CAP, RIM) * after_ok[:RIM]

    def run(block):
        rows = act_rows * block

        def fill_one(b, c):
            fill(block, b)
            return c

        lax.fori_loop(0, block, fill_one, 0, unroll=2)
        for p in range(pieces):
            for q in range(KPRE):
                taps[pl.ds(p * rows, rows), pl.ds(q * LANES, LANES)] = win[p, pl.ds(q * block, rows), :].astype(
                    jnp.bfloat16
                )

        load_pre(False)

        if not rims:
            zeros[...] = jnp.zeros_like(zeros)

            def clear(i, c):
                @pl.when(plan[i] < 0)
                def _():
                    copy_of(zeros, out.at[i], zero_sem.at[i]).start()

                return c

            lax.fori_loop(0, n_slots, clear, 0)

        def conv_chunk(n, c):
            def vector(i):
                return vectors[:, pl.ds(pl.multiple_of(i * channels + n * STEP, STEP), STEP)]

            cols = pl.ds(pl.multiple_of(n * STEP, STEP), STEP)
            bias = vector(0)
            scale = vector(1) * (1.0 / jnp.pi)
            inverse = 1.0 / vector(2)
            for p in range(pieces):
                sums = jnp.dot(taps[pl.ds(p * rows, rows), :], wp[:, cols], preferred_element_type=jnp.float32)
                mask = msk[p, pl.ds(3 * block, rows), :]
                hidden = jnp.concatenate([mask] * tiles, axis=1) * (sums + bias)
                turns = hidden * scale
                rest_of = turns - jnp.floor(turns + 0.5)
                u = rest_of * rest_of
                poly = SIN2[-1] * u + SIN2[-2]
                for coef in SIN2[-3::-1]:
                    poly = poly * u + coef
                acts[pl.ds(p * rows, rows), cols] = (hidden + u * poly * inverse).astype(jnp.bfloat16)
            return c

        lax.fori_loop(0, channels // STEP, conv_chunk, 0, unroll=3)

        def acts_from(shift):
            picked = [acts[pl.ds(p * rows + shift * block, frames * block), :] for p in range(pieces)]
            return picked[0] if pieces == 1 else jnp.concatenate(picked, axis=0)

        def up_part(n, c):
            load_taps(n, False)
            for r in range(UP):
                sums = vectors[:, pl.ds(pl.multiple_of(3 * channels + n * STEP, STEP), STEP)]
                for tap, shift in zip(phases[r], (1, 0 if r < UP // 2 else 2)):
                    cols = pl.ds(pl.multiple_of(tap * width + n * STEP, STEP), STEP)
                    sums = sums + jnp.dot(acts_from(shift), wu[:, cols], preferred_element_type=jnp.float32)
                for p in range(pieces):
                    for j in range(frames):
                        mask = msk[p, pl.ds((j + 4) * block, block), :]
                        here = (p * frames + j) * block
                        for half in range(tiles):
                            rows32[
                                n * tiles + half, pl.ds(p * block * pitch + UP * j + r, block, stride=pitch), :
                            ] = mask * sums[here : here + block, half * LANES : (half + 1) * LANES]
            return c

        lax.fori_loop(0, parts, up_part, 0)

        def send(b, c):
            for p in range(pieces):
                for n in range(width // LANES):
                    stage[p, b, :, n * LANES : (n + 1) * LANES] = rows32[
                        n, pl.ds(pl.multiple_of((p * block + b) * pitch, 8), span), :
                    ].astype(jnp.bfloat16)

            @pl.when(b < found)
            def _():
                for p in range(pieces):
                    copy_of(stage.at[p, b], out.at[slots[b], pl.ds(UP * starts[p], span)], out_sem.at[p, b]).start()

            return c

        lax.fori_loop(0, block, send, 0)

    for units in range(1, 5):

        @pl.when((found > 16 * (units - 1)) & (found <= 16 * units))
        def _(units=units):
            run(16 * units)

    @pl.when(found == 0)
    def _():
        load_pre(False)
        for n in range(parts):
            load_taps(n, False)
        if not rims:
            zeros[...] = jnp.zeros_like(zeros)

            def clear(i, c):
                copy_of(zeros, out.at[i], zero_sem.at[i]).start()
                return c

            lax.fori_loop(0, n_slots, clear, 0)

    def settle(b, c):
        for p in range(pieces):
            copy_of(stage.at[p, b], out.at[0, pl.ds(0, span)], out_sem.at[p, b]).wait()
        return c

    lax.fori_loop(0, found, settle, 0)

    if not rims:

        def cleared(i, c):
            @pl.when(plan[i] < 0)
            def _():
                copy_of(zeros, out.at[i], zero_sem.at[i]).wait()

            return c

        lax.fori_loop(0, n_slots, cleared, 0)


def vocode(starts, frames, home, waves, plan, features, w_pre, w_up, vectors):
    rims = home is not None
    pieces = len(starts)
    n_slots, seg, feat = features.shape
    channels = w_pre.shape[1]
    width = w_up.shape[1] // (2 * UP)
    span = UP * frames
    smem = pl.BlockSpec(memory_space=pltpu.SMEM)
    vmem = pl.BlockSpec(memory_space=pltpu.VMEM)
    hbm = pl.BlockSpec(memory_space=pl.ANY)
    operands = [plan, features]
    specs = [smem, vmem]
    if rims:
        operands.append(home)
        specs.append(vmem)
    operands += [w_pre, w_up, vectors]
    specs += [hbm, hbm, vmem]
    aliases = {}
    if rims:
        aliases = {len(operands): 0}
        operands.append(waves)
        specs.append(hbm)
    return pl.pallas_call(
        functools.partial(vocode_kernel, starts, frames, rims),
        out_shape=jax.ShapeDtypeStruct((n_slots, UP * seg, width), jnp.bfloat16),
        in_specs=specs,
        out_specs=hbm,
        input_output_aliases=aliases,
        scratch_shapes=[
            pltpu.VMEM(w_pre.shape, jnp.bfloat16),
            pltpu.VMEM(w_up.shape, jnp.bfloat16),
            pltpu.VMEM((pieces, (frames + 8) * n_slots, feat), jnp.float32),
            pltpu.VMEM((pieces, (frames + 8) * n_slots, feat), jnp.float32),
            pltpu.VMEM((pieces * (frames + 2) * n_slots, KPRE * feat), jnp.bfloat16),
            pltpu.VMEM((pieces * (frames + 2) * n_slots, channels), jnp.bfloat16),
            pltpu.VMEM((width // LANES, pieces * n_slots * (span + 8), LANES), jnp.float32),
            pltpu.VMEM((pieces, n_slots, span, width), jnp.bfloat16),
            pltpu.VMEM((16, LANES) if rims else (UP * seg, width), jnp.bfloat16),
            pltpu.SMEM((n_slots + 1,), jnp.int32),
            pltpu.SMEM((n_slots + 1,), jnp.int32),
            pltpu.SMEM((17,), jnp.int32),
            pltpu.SemaphoreType.DMA((width // STEP + 1, 2 * UP)),
            pltpu.SemaphoreType.DMA((pieces, n_slots)),
            pltpu.SemaphoreType.DMA((n_slots,)),
        ],
        compiler_params=pltpu.CompilerParams(vmem_limit_bytes=58 * 2**20),
        cost_estimate=pl.CostEstimate(
            flops=2 * 48 * pieces * frames * 2 * channels * UP * width,
            bytes_accessed=2 * (w_up.size + w_pre.size + 48 * pieces * span * width),
            transcendentals=0,
        ),
        name="edges" if rims else "inner",
    )(*operands)


def one_hot_rows(match, values):
    rows = jnp.dot(match.astype(jnp.bfloat16), values.reshape(values.shape[0], -1), preferred_element_type=jnp.float32)
    return rows.astype(jnp.bfloat16)


def packed(features, target):
    n_slots, seg, feat = features.shape
    used = target >= 0
    worker = jnp.where(used, target // 32, -1)
    order = jnp.arange(n_slots, dtype=jnp.int32)
    rank = jnp.sum(((worker[:, None] == worker[None, :]) & (order[:, None] < order[None, :])).astype(jnp.int32), axis=0)
    slot = target % 32 + 1

    def sorted_rows(worker_of, values):
        row = jnp.where(used, worker_of * CAP + rank, -1)
        select = row[None, :] == jnp.arange(16 * CAP, dtype=jnp.int32)[:, None]
        code = jnp.sum(jnp.where(select, slot[None, :], 0), axis=1).astype(jnp.bfloat16)
        return one_hot_rows(select, values).reshape(16, CAP, RIM, feat), code.reshape(16, CAP)

    heads, head_code = sorted_rows(worker, features[:, :RIM])
    tails, tail_code = sorted_rows((worker + 1) % 16, features[:, seg - RIM :])
    codes = jnp.concatenate([tail_code, head_code], axis=1)
    codes = jnp.broadcast_to(codes[:, None, :, None], (16, 1, 2 * CAP, feat))
    return jnp.concatenate([jnp.concatenate([tails, heads], axis=2), codes], axis=1)


def swapped(got):
    def codes(first):
        return got[:, CAP, first : first + CAP, 0].astype(jnp.int32).reshape(-1)

    def entries(first):
        return got[:, :CAP, first : first + RIM].reshape(got.shape[0] * CAP, -1)

    tail_code, head_code = codes(0), codes(RIM)
    match = (tail_code[:, None] == head_code[None, :]) & (tail_code[:, None] > 0)
    shape = (got.shape[0], CAP, RIM, got.shape[3])
    heads = one_hot_rows(match, entries(RIM)).reshape(shape)
    tails = one_hot_rows(match.T, entries(0)).reshape(shape)
    return jnp.concatenate([heads, tails], axis=2)


def from_groups(own):
    gen, count = lax.axis_index("gen"), lax.axis_size("gen")
    lower = lax.ppermute(own, "gen", [(g, (g + 1) % count) for g in range(count)])[:, :RIM]
    upper = lax.ppermute(own, "gen", [(g, (g - 1) % count) for g in range(count)])[:, RIM:]
    tail_code, head_code = lower[CAP].astype(jnp.float32), upper[CAP].astype(jnp.float32)
    stepped = jnp.where(tail_code == 32, 1.0, tail_code + 1)
    tail_code = jnp.where((gen == 0) & (tail_code > 0), stepped, tail_code)
    stepped = jnp.where(head_code == 1, 32.0, head_code - 1)
    head_code = jnp.where((gen == count - 1) & (head_code > 0), stepped, head_code)
    codes = jnp.concatenate([tail_code, head_code], axis=0).astype(own.dtype)
    return jnp.concatenate([jnp.concatenate([lower[:CAP], upper[:CAP]], axis=1), codes[None]], axis=0)


def on_device(features, target, extents, w_pre, biases, snake_params, w_up, up_bias):
    rims = packed(features, target)
    plan = jnp.concatenate([target, extents.reshape(-1)])
    far = from_groups(lax.optimization_barrier((rims[0], plan))[0])
    got = lax.all_to_all(rims, "voc", split_axis=0, concat_axis=0, tiled=True)
    back = jnp.concatenate([swapped(got), jnp.broadcast_to(far, rims.shape)], axis=1)
    home = lax.all_to_all(back, "voc", split_axis=0, concat_axis=0, tiled=True)
    vectors = jnp.concatenate([biases, snake_params.reshape(-1), up_bias])[None, :]
    rest = (plan, features, w_pre, w_up, vectors)
    waves = vocode((RIM,), 16, None, None, *rest)
    return vocode((0, 20), 4, home, waves, *rest)


def solution(mesh):
    split = P(("gen", "voc"))
    return jax.shard_map(
        on_device,
        mesh=mesh,
        in_specs=(split, split, split, P(), P(), P(), P(), P()),
        out_specs=split,
        check_vma=False,
    )
```

```python
import functools

import jax
import jax.numpy as jnp
from jax import lax
from jax.experimental import pallas as pl
from jax.experimental.pallas import tpu as pltpu
from jax.sharding import PartitionSpec as P

UP = 4
KPRE = 7
RIM = 4
CAP = 4
LANES = 128
STEP = 256

SIN2 = (9.869604311707747, -32.46967117172015, 42.72719633651888, -30.101465841328583, 13.050098920339147, -3.3565926218240247)


def copy_of(src, dst, sem):
    return pltpu.make_async_copy(src, dst, sem)


def vocode_kernel(starts, frames, rims, plan, features, *rest):
    if rims:
        home, w_pre, w_up, vectors, _, out = rest[:6]
        scratch = rest[6:]
    else:
        home = None
        w_pre, w_up, vectors, out = rest[:4]
        scratch = rest[4:]
    (wp, wu, win, msk, taps, acts, rows32, stage, zeros, slots, ranks, counts, w_sem, out_sem, zero_sem) = scratch
    pieces = len(starts)
    act_rows = frames + 2
    win_rows = frames + 8
    seg = features.shape[1]
    channels = wp.shape[1]
    width = wu.shape[1] // (2 * UP)
    n_slots = features.shape[0]
    span = UP * frames
    pitch = span + 8
    parts = width // STEP
    tiles = STEP // LANES

    phases = tuple((r + UP // 2, r + UP + UP // 2 if r < UP // 2 else r - UP // 2) for r in range(UP))

    def load_taps(n, start):
        for tap in sum(phases, ()):
            cols = pl.ds(pl.multiple_of(tap * width + n * STEP, STEP), STEP)
            copy = copy_of(w_up.at[:, cols], wu.at[:, cols], w_sem.at[n, tap])
            copy.start() if start else copy.wait()

    def load_pre(start):
        copy = copy_of(w_pre, wp, w_sem.at[parts, 0])
        copy.start() if start else copy.wait()

    load_pre(True)
    for n in range(parts):
        load_taps(n, True)
    for v in range(17):
        counts[v] = 0
    slots[0] = 0
    ranks[0] = 0

    def scan(i, found):
        code = plan[i]
        used = code >= 0
        slots[found] = i
        if rims:
            worker = jnp.where(used, lax.shift_right_logical(code, 5), 16)
            rank = counts[worker]
            ranks[found] = rank
            counts[worker] = rank + 1
        return found + used.astype(jnp.int32)

    found = lax.fori_loop(0, n_slots, scan, jnp.int32(0), unroll=8)

    cell = lax.broadcasted_iota(jnp.int32, (seg, LANES), 0)
    rim_cell = lax.broadcasted_iota(jnp.int32, (2 * RIM, LANES), 0)

    def fill(block, b):
        c = jnp.minimum(b, found - 1)
        slot = slots[c]
        own = (cell < plan[n_slots + slot * 3]).astype(jnp.float32)
        values = features[slot].astype(jnp.float32) * own
        if not rims:
            win[0, pl.ds(b, seg, stride=block), :] = values
            msk[0, pl.ds(b, seg, stride=block), :] = own
        else:
            at = RIM * block + b
            inner = win_rows - RIM
            win[0, pl.ds(at, inner, stride=block), :] = values[:inner]
            msk[0, pl.ds(at, inner, stride=block), :] = own[:inner]
            win[1, pl.ds(b, inner, stride=block), :] = values[seg - inner :]
            msk[1, pl.ds(b, inner, stride=block), :] = own[seg - inner :]
            worker = lax.shift_right_logical(plan[slot], 5)
            rank = ranks[c]
            before_ok = (rim_cell - RIM + seg - RIM < plan[n_slots + slot * 3 + 1]).astype(jnp.float32)
            after_ok = (rim_cell < plan[n_slots + slot * 3 + 2]).astype(jnp.float32)
            before = home[worker, rank].astype(jnp.float32) * before_ok
            after = home[(worker + 1) & 15, rank].astype(jnp.float32) * after_ok
            win[0, pl.ds(b, RIM, stride=block), :] = before[RIM:]
            msk[0, pl.ds(b, RIM, stride=block), :] = before_ok[RIM:]
            tail = inner * block + b
            win[1, pl.ds(tail, RIM, stride=block), :] = after[:RIM]
            msk[1, pl.ds(tail, RIM, stride=block), :] = after_ok[:RIM]

            def far(row, rows_from):
                code = (plan[slot] & 31).astype(jnp.float32) + 1.0

                def look(k, total):
                    codes = home[k, 2 * CAP].astype(jnp.float32)
                    for e in range(CAP):
                        entry = home[k, CAP + e].astype(jnp.float32)
                        total = total + jnp.where(codes[row + e : row + e + 1] == code, entry, 0.0)
                    return total

                total = lax.fori_loop(0, home.shape[0], look, jnp.zeros((2 * RIM, LANES), jnp.float32), unroll=2)
                return total[rows_from : rows_from + RIM]

            @pl.when(worker == 0)
            def _():
                win[0, pl.ds(b, RIM, stride=block), :] = far(0, 0) * before_ok[RIM:]

            @pl.when(worker == 15)
            def _():
                win[1, pl.ds(tail, RIM, stride=block), :] = far(CAP, RIM) * after_ok[:RIM]

    def run(block):
        rows = act_rows * block

        def fill_one(b, c):
            fill(block, b)
            return c

        lax.fori_loop(0, block, fill_one, 0, unroll=2)
        for p in range(pieces):
            for q in range(KPRE):
                taps[pl.ds(p * rows, rows), pl.ds(q * LANES, LANES)] = win[p, pl.ds(q * block, rows), :].astype(
                    jnp.bfloat16
                )

        load_pre(False)

        if not rims:
            zeros[...] = jnp.zeros_like(zeros)

            def clear(i, c):
                @pl.when(plan[i] < 0)
                def _():
                    copy_of(zeros, out.at[i], zero_sem.at[i]).start()

                return c

            lax.fori_loop(0, n_slots, clear, 0)

        def conv_chunk(n, c):
            def vector(i):
                return vectors[:, pl.ds(pl.multiple_of(i * channels + n * STEP, STEP), STEP)]

            cols = pl.ds(pl.multiple_of(n * STEP, STEP), STEP)
            bias = vector(0)
            scale = vector(1) * (1.0 / jnp.pi)
            inverse = 1.0 / vector(2)
            for p in range(pieces):
                sums = jnp.dot(taps[pl.ds(p * rows, rows), :], wp[:, cols], preferred_element_type=jnp.float32)
                mask = msk[p, pl.ds(3 * block, rows), :]
                hidden = jnp.concatenate([mask] * tiles, axis=1) * (sums + bias)
                turns = hidden * scale
                rest_of = turns - jnp.floor(turns + 0.5)
                u = rest_of * rest_of
                poly = SIN2[-1] * u + SIN2[-2]
                for coef in SIN2[-3::-1]:
                    poly = poly * u + coef
                acts[pl.ds(p * rows, rows), cols] = (hidden + u * poly * inverse).astype(jnp.bfloat16)
            return c

        lax.fori_loop(0, channels // STEP, conv_chunk, 0, unroll=2)

        def acts_from(shift):
            picked = [acts[pl.ds(p * rows + shift * block, frames * block), :] for p in range(pieces)]
            return picked[0] if pieces == 1 else jnp.concatenate(picked, axis=0)

        def up_part(n, c):
            load_taps(n, False)
            for r in range(UP):
                sums = vectors[:, pl.ds(pl.multiple_of(3 * channels + n * STEP, STEP), STEP)]
                for tap, shift in zip(phases[r], (1, 0 if r < UP // 2 else 2)):
                    cols = pl.ds(pl.multiple_of(tap * width + n * STEP, STEP), STEP)
                    sums = sums + jnp.dot(acts_from(shift), wu[:, cols], preferred_element_type=jnp.float32)
                for p in range(pieces):
                    for j in range(frames):
                        mask = msk[p, pl.ds((j + 4) * block, block), :]
                        here = (p * frames + j) * block
                        for half in range(tiles):
                            rows32[
                                n * tiles + half, pl.ds(p * block * pitch + UP * j + r, block, stride=pitch), :
                            ] = mask * sums[here : here + block, half * LANES : (half + 1) * LANES]
            return c

        lax.fori_loop(0, parts, up_part, 0)

        def send(b, c):
            for p in range(pieces):
                for n in range(width // LANES):
                    stage[p, b, :, n * LANES : (n + 1) * LANES] = rows32[
                        n, pl.ds(pl.multiple_of((p * block + b) * pitch, 8), span), :
                    ].astype(jnp.bfloat16)

            @pl.when(b < found)
            def _():
                for p in range(pieces):
                    copy_of(stage.at[p, b], out.at[slots[b], pl.ds(UP * starts[p], span)], out_sem.at[p, b]).start()

            return c

        lax.fori_loop(0, block, send, 0)

    for units in range(1, 5):

        @pl.when((found > 16 * (units - 1)) & (found <= 16 * units))
        def _(units=units):
            run(16 * units)

    @pl.when(found == 0)
    def _():
        load_pre(False)
        for n in range(parts):
            load_taps(n, False)
        if not rims:
            zeros[...] = jnp.zeros_like(zeros)

            def clear(i, c):
                copy_of(zeros, out.at[i], zero_sem.at[i]).start()
                return c

            lax.fori_loop(0, n_slots, clear, 0)

    def settle(b, c):
        for p in range(pieces):
            copy_of(stage.at[p, b], out.at[0, pl.ds(0, span)], out_sem.at[p, b]).wait()
        return c

    lax.fori_loop(0, found, settle, 0)

    if not rims:

        def cleared(i, c):
            @pl.when(plan[i] < 0)
            def _():
                copy_of(zeros, out.at[i], zero_sem.at[i]).wait()

            return c

        lax.fori_loop(0, n_slots, cleared, 0)


def vocode(starts, frames, home, waves, plan, features, w_pre, w_up, vectors):
    rims = home is not None
    pieces = len(starts)
    n_slots, seg, feat = features.shape
    channels = w_pre.shape[1]
    width = w_up.shape[1] // (2 * UP)
    span = UP * frames
    smem = pl.BlockSpec(memory_space=pltpu.SMEM)
    vmem = pl.BlockSpec(memory_space=pltpu.VMEM)
    hbm = pl.BlockSpec(memory_space=pl.ANY)
    operands = [plan, features]
    specs = [smem, vmem]
    if rims:
        operands.append(home)
        specs.append(vmem)
    operands += [w_pre, w_up, vectors]
    specs += [hbm, hbm, vmem]
    aliases = {}
    if rims:
        aliases = {len(operands): 0}
        operands.append(waves)
        specs.append(hbm)
    return pl.pallas_call(
        functools.partial(vocode_kernel, starts, frames, rims),
        out_shape=jax.ShapeDtypeStruct((n_slots, UP * seg, width), jnp.bfloat16),
        in_specs=specs,
        out_specs=hbm,
        input_output_aliases=aliases,
        scratch_shapes=[
            pltpu.VMEM(w_pre.shape, jnp.bfloat16),
            pltpu.VMEM(w_up.shape, jnp.bfloat16),
            pltpu.VMEM((pieces, (frames + 8) * n_slots, feat), jnp.float32),
            pltpu.VMEM((pieces, (frames + 8) * n_slots, feat), jnp.float32),
            pltpu.VMEM((pieces * (frames + 2) * n_slots, KPRE * feat), jnp.bfloat16),
            pltpu.VMEM((pieces * (frames + 2) * n_slots, channels), jnp.bfloat16),
            pltpu.VMEM((width // LANES, pieces * n_slots * (span + 8), LANES), jnp.float32),
            pltpu.VMEM((pieces, n_slots, span, width), jnp.bfloat16),
            pltpu.VMEM((16, LANES) if rims else (UP * seg, width), jnp.bfloat16),
            pltpu.SMEM((n_slots + 1,), jnp.int32),
            pltpu.SMEM((n_slots + 1,), jnp.int32),
            pltpu.SMEM((17,), jnp.int32),
            pltpu.SemaphoreType.DMA((width // STEP + 1, 2 * UP)),
            pltpu.SemaphoreType.DMA((pieces, n_slots)),
            pltpu.SemaphoreType.DMA((n_slots,)),
        ],
        compiler_params=pltpu.CompilerParams(vmem_limit_bytes=58 * 2**20),
        cost_estimate=pl.CostEstimate(
            flops=2 * 48 * pieces * frames * 2 * channels * UP * width,
            bytes_accessed=2 * (w_up.size + w_pre.size + 48 * pieces * span * width),
            transcendentals=0,
        ),
        name="edges" if rims else "inner",
    )(*operands)


def one_hot_rows(match, values):
    rows = jnp.dot(match.astype(jnp.bfloat16), values.reshape(values.shape[0], -1), preferred_element_type=jnp.float32)
    return rows.astype(jnp.bfloat16)


def packed(features, target):
    n_slots, seg, feat = features.shape
    used = target >= 0
    worker = jnp.where(used, target // 32, -1)
    order = jnp.arange(n_slots, dtype=jnp.int32)
    rank = jnp.sum(((worker[:, None] == worker[None, :]) & (order[:, None] < order[None, :])).astype(jnp.int32), axis=0)
    slot = target % 32 + 1

    def sorted_rows(worker_of, values):
        row = jnp.where(used, worker_of * CAP + rank, -1)
        select = row[None, :] == jnp.arange(16 * CAP, dtype=jnp.int32)[:, None]
        code = jnp.sum(jnp.where(select, slot[None, :], 0), axis=1).astype(jnp.bfloat16)
        return one_hot_rows(select, values).reshape(16, CAP, RIM, feat), code.reshape(16, CAP)

    heads, head_code = sorted_rows(worker, features[:, :RIM])
    tails, tail_code = sorted_rows((worker + 1) % 16, features[:, seg - RIM :])
    codes = jnp.concatenate([tail_code, head_code], axis=1)
    codes = jnp.broadcast_to(codes[:, None, :, None], (16, 1, 2 * CAP, feat))
    return jnp.concatenate([jnp.concatenate([tails, heads], axis=2), codes], axis=1)


def swapped(got):
    def codes(first):
        return got[:, CAP, first : first + CAP, 0].astype(jnp.int32).reshape(-1)

    def entries(first):
        return got[:, :CAP, first : first + RIM].reshape(got.shape[0] * CAP, -1)

    tail_code, head_code = codes(0), codes(RIM)
    match = (tail_code[:, None] == head_code[None, :]) & (tail_code[:, None] > 0)
    shape = (got.shape[0], CAP, RIM, got.shape[3])
    heads = one_hot_rows(match, entries(RIM)).reshape(shape)
    tails = one_hot_rows(match.T, entries(0)).reshape(shape)
    return jnp.concatenate([heads, tails], axis=2)


def from_groups(own):
    gen, count = lax.axis_index("gen"), lax.axis_size("gen")
    lower = lax.ppermute(own, "gen", [(g, (g + 1) % count) for g in range(count)])[:, :RIM]
    upper = lax.ppermute(own, "gen", [(g, (g - 1) % count) for g in range(count)])[:, RIM:]
    tail_code, head_code = lower[CAP].astype(jnp.float32), upper[CAP].astype(jnp.float32)
    stepped = jnp.where(tail_code == 32, 1.0, tail_code + 1)
    tail_code = jnp.where((gen == 0) & (tail_code > 0), stepped, tail_code)
    stepped = jnp.where(head_code == 1, 32.0, head_code - 1)
    head_code = jnp.where((gen == count - 1) & (head_code > 0), stepped, head_code)
    codes = jnp.concatenate([tail_code, head_code], axis=0).astype(own.dtype)
    return jnp.concatenate([jnp.concatenate([lower[:CAP], upper[:CAP]], axis=1), codes[None]], axis=0)


def on_device(features, target, extents, w_pre, biases, snake_params, w_up, up_bias):
    rims = packed(features, target)
    plan = jnp.concatenate([target, extents.reshape(-1)])
    far = from_groups(lax.optimization_barrier((rims[0], plan))[0])
    got = lax.all_to_all(rims, "voc", split_axis=0, concat_axis=0, tiled=True)
    back = jnp.concatenate([swapped(got), jnp.broadcast_to(far, rims.shape)], axis=1)
    home = lax.all_to_all(back, "voc", split_axis=0, concat_axis=0, tiled=True)
    vectors = jnp.concatenate([biases, snake_params.reshape(-1), up_bias])[None, :]
    rest = (plan, features, w_pre, w_up, vectors)
    waves = vocode((RIM,), 16, None, None, *rest)
    return vocode((0, 20), 4, home, waves, *rest)


def solution(mesh):
    split = P(("gen", "voc"))
    return jax.shard_map(
        on_device,
        mesh=mesh,
        in_specs=(split, split, split, P(), P(), P(), P(), P()),
        out_specs=split,
        check_vma=False,
    )
```

```python
import functools

import jax
import jax.numpy as jnp
from jax import lax
from jax.experimental import pallas as pl
from jax.experimental.pallas import tpu as pltpu
from jax.sharding import PartitionSpec as P

UP = 4
KPRE = 7
RIM = 4
CAP = 4
LANES = 128
STEP = 256

SIN2 = (9.869604311707747, -32.46967117172015, 42.72719633651888, -30.101465841328583, 13.050098920339147, -3.3565926218240247)


def copy_of(src, dst, sem):
    return pltpu.make_async_copy(src, dst, sem)


def vocode_kernel(starts, frames, rims, plan, features, *rest):
    if rims:
        home, w_pre, w_up, vectors, _, out = rest[:6]
        scratch = rest[6:]
    else:
        home = None
        w_pre, w_up, vectors, out = rest[:4]
        scratch = rest[4:]
    (wp, wu, win, msk, taps, acts, rows32, stage, zeros, slots, ranks, counts, w_sem, out_sem, zero_sem) = scratch
    pieces = len(starts)
    act_rows = frames + 2
    win_rows = frames + 8
    seg = features.shape[1]
    channels = wp.shape[1]
    width = wu.shape[1] // (2 * UP)
    n_slots = features.shape[0]
    span = UP * frames
    pitch = span + 8
    parts = width // STEP
    tiles = STEP // LANES

    phases = tuple((r + UP // 2, r + UP + UP // 2 if r < UP // 2 else r - UP // 2) for r in range(UP))

    def load_taps(n, start):
        for tap in sum(phases, ()):
            cols = pl.ds(pl.multiple_of(tap * width + n * STEP, STEP), STEP)
            copy = copy_of(w_up.at[:, cols], wu.at[:, cols], w_sem.at[n, tap])
            copy.start() if start else copy.wait()

    def load_pre(start):
        copy = copy_of(w_pre, wp, w_sem.at[parts, 0])
        copy.start() if start else copy.wait()

    load_pre(True)
    for n in range(parts):
        load_taps(n, True)
    for v in range(17):
        counts[v] = 0
    slots[0] = 0
    ranks[0] = 0

    def scan(i, found):
        code = plan[i]
        used = code >= 0
        slots[found] = i
        if rims:
            worker = jnp.where(used, lax.shift_right_logical(code, 5), 16)
            rank = counts[worker]
            ranks[found] = rank
            counts[worker] = rank + 1
        return found + used.astype(jnp.int32)

    found = lax.fori_loop(0, n_slots, scan, jnp.int32(0), unroll=8)

    cell = lax.broadcasted_iota(jnp.int32, (seg, LANES), 0)
    rim_cell = lax.broadcasted_iota(jnp.int32, (2 * RIM, LANES), 0)

    def fill(block, b):
        c = jnp.minimum(b, found - 1)
        slot = slots[c]
        own = (cell < plan[n_slots + slot * 3]).astype(jnp.float32)
        values = features[slot].astype(jnp.float32) * own
        if not rims:
            win[0, pl.ds(b, seg, stride=block), :] = values
            msk[0, pl.ds(b, seg, stride=block), :] = own
        else:
            at = RIM * block + b
            inner = win_rows - RIM
            win[0, pl.ds(at, inner, stride=block), :] = values[:inner]
            msk[0, pl.ds(at, inner, stride=block), :] = own[:inner]
            win[1, pl.ds(b, inner, stride=block), :] = values[seg - inner :]
            msk[1, pl.ds(b, inner, stride=block), :] = own[seg - inner :]
            worker = lax.shift_right_logical(plan[slot], 5)
            rank = ranks[c]
            before_ok = (rim_cell - RIM + seg - RIM < plan[n_slots + slot * 3 + 1]).astype(jnp.float32)
            after_ok = (rim_cell < plan[n_slots + slot * 3 + 2]).astype(jnp.float32)
            before = home[worker, rank].astype(jnp.float32) * before_ok
            after = home[(worker + 1) & 15, rank].astype(jnp.float32) * after_ok
            win[0, pl.ds(b, RIM, stride=block), :] = before[RIM:]
            msk[0, pl.ds(b, RIM, stride=block), :] = before_ok[RIM:]
            tail = inner * block + b
            win[1, pl.ds(tail, RIM, stride=block), :] = after[:RIM]
            msk[1, pl.ds(tail, RIM, stride=block), :] = after_ok[:RIM]

            def far(row, rows_from):
                code = (plan[slot] & 31).astype(jnp.float32) + 1.0

                def look(k, total):
                    codes = home[k, 2 * CAP].astype(jnp.float32)
                    for e in range(CAP):
                        entry = home[k, CAP + e].astype(jnp.float32)
                        total = total + jnp.where(codes[row + e : row + e + 1] == code, entry, 0.0)
                    return total

                total = lax.fori_loop(0, home.shape[0], look, jnp.zeros((2 * RIM, LANES), jnp.float32), unroll=4)
                return total[rows_from : rows_from + RIM]

            @pl.when(worker == 0)
            def _():
                win[0, pl.ds(b, RIM, stride=block), :] = far(0, 0) * before_ok[RIM:]

            @pl.when(worker == 15)
            def _():
                win[1, pl.ds(tail, RIM, stride=block), :] = far(CAP, RIM) * after_ok[:RIM]

    def run(block):
        rows = act_rows * block

        def fill_one(b, c):
            fill(block, b)
            return c

        lax.fori_loop(0, block, fill_one, 0, unroll=2)
        for p in range(pieces):
            for q in range(KPRE):
                taps[pl.ds(p * rows, rows), pl.ds(q * LANES, LANES)] = win[p, pl.ds(q * block, rows), :].astype(
                    jnp.bfloat16
                )

        load_pre(False)

        if not rims:
            zeros[...] = jnp.zeros_like(zeros)

            def clear(i, c):
                @pl.when(plan[i] < 0)
                def _():
                    copy_of(zeros, out.at[i], zero_sem.at[i]).start()

                return c

            lax.fori_loop(0, n_slots, clear, 0)

        def conv_chunk(n, c):
            def vector(i):
                return vectors[:, pl.ds(pl.multiple_of(i * channels + n * STEP, STEP), STEP)]

            cols = pl.ds(pl.multiple_of(n * STEP, STEP), STEP)
            bias = vector(0)
            scale = vector(1) * (1.0 / jnp.pi)
            inverse = 1.0 / vector(2)
            for p in range(pieces):
                sums = jnp.dot(taps[pl.ds(p * rows, rows), :], wp[:, cols], preferred_element_type=jnp.float32)
                mask = msk[p, pl.ds(3 * block, rows), :]
                hidden = jnp.concatenate([mask] * tiles, axis=1) * (sums + bias)
                turns = hidden * scale
                rest_of = turns - jnp.floor(turns + 0.5)
                u = rest_of * rest_of
                poly = SIN2[-1] * u + SIN2[-2]
                for coef in SIN2[-3::-1]:
                    poly = poly * u + coef
                acts[pl.ds(p * rows, rows), cols] = (hidden + u * poly * inverse).astype(jnp.bfloat16)
            return c

        lax.fori_loop(0, channels // STEP, conv_chunk, 0, unroll=2)

        def acts_from(shift):
            picked = [acts[pl.ds(p * rows + shift * block, frames * block), :] for p in range(pieces)]
            return picked[0] if pieces == 1 else jnp.concatenate(picked, axis=0)

        def up_part(n, c):
            load_taps(n, False)
            for r in range(UP):
                sums = vectors[:, pl.ds(pl.multiple_of(3 * channels + n * STEP, STEP), STEP)]
                for tap, shift in zip(phases[r], (1, 0 if r < UP // 2 else 2)):
                    cols = pl.ds(pl.multiple_of(tap * width + n * STEP, STEP), STEP)
                    sums = sums + jnp.dot(acts_from(shift), wu[:, cols], preferred_element_type=jnp.float32)
                for p in range(pieces):
                    for j in range(frames):
                        mask = msk[p, pl.ds((j + 4) * block, block), :]
                        here = (p * frames + j) * block
                        for half in range(tiles):
                            rows32[
                                n * tiles + half, pl.ds(p * block * pitch + UP * j + r, block, stride=pitch), :
                            ] = mask * sums[here : here + block, half * LANES : (half + 1) * LANES]
            return c

        lax.fori_loop(0, parts, up_part, 0)

        def send(b, c):
            for p in range(pieces):
                for n in range(width // LANES):
                    stage[p, b, :, n * LANES : (n + 1) * LANES] = rows32[
                        n, pl.ds(pl.multiple_of((p * block + b) * pitch, 8), span), :
                    ].astype(jnp.bfloat16)

            @pl.when(b < found)
            def _():
                for p in range(pieces):
                    copy_of(stage.at[p, b], out.at[slots[b], pl.ds(UP * starts[p], span)], out_sem.at[p, b]).start()

            return c

        lax.fori_loop(0, block, send, 0)

    for units in range(1, 5):

        @pl.when((found > 16 * (units - 1)) & (found <= 16 * units))
        def _(units=units):
            run(16 * units)

    @pl.when(found == 0)
    def _():
        load_pre(False)
        for n in range(parts):
            load_taps(n, False)
        if not rims:
            zeros[...] = jnp.zeros_like(zeros)

            def clear(i, c):
                copy_of(zeros, out.at[i], zero_sem.at[i]).start()
                return c

            lax.fori_loop(0, n_slots, clear, 0)

    def settle(b, c):
        for p in range(pieces):
            copy_of(stage.at[p, b], out.at[0, pl.ds(0, span)], out_sem.at[p, b]).wait()
        return c

    lax.fori_loop(0, found, settle, 0)

    if not rims:

        def cleared(i, c):
            @pl.when(plan[i] < 0)
            def _():
                copy_of(zeros, out.at[i], zero_sem.at[i]).wait()

            return c

        lax.fori_loop(0, n_slots, cleared, 0)


def vocode(starts, frames, home, waves, plan, features, w_pre, w_up, vectors):
    rims = home is not None
    pieces = len(starts)
    n_slots, seg, feat = features.shape
    channels = w_pre.shape[1]
    width = w_up.shape[1] // (2 * UP)
    span = UP * frames
    smem = pl.BlockSpec(memory_space=pltpu.SMEM)
    vmem = pl.BlockSpec(memory_space=pltpu.VMEM)
    hbm = pl.BlockSpec(memory_space=pl.ANY)
    operands = [plan, features]
    specs = [smem, vmem]
    if rims:
        operands.append(home)
        specs.append(vmem)
    operands += [w_pre, w_up, vectors]
    specs += [hbm, hbm, vmem]
    aliases = {}
    if rims:
        aliases = {len(operands): 0}
        operands.append(waves)
        specs.append(hbm)
    return pl.pallas_call(
        functools.partial(vocode_kernel, starts, frames, rims),
        out_shape=jax.ShapeDtypeStruct((n_slots, UP * seg, width), jnp.bfloat16),
        in_specs=specs,
        out_specs=hbm,
        input_output_aliases=aliases,
        scratch_shapes=[
            pltpu.VMEM(w_pre.shape, jnp.bfloat16),
            pltpu.VMEM(w_up.shape, jnp.bfloat16),
            pltpu.VMEM((pieces, (frames + 8) * n_slots, feat), jnp.float32),
            pltpu.VMEM((pieces, (frames + 8) * n_slots, feat), jnp.float32),
            pltpu.VMEM((pieces * (frames + 2) * n_slots, KPRE * feat), jnp.bfloat16),
            pltpu.VMEM((pieces * (frames + 2) * n_slots, channels), jnp.bfloat16),
            pltpu.VMEM((width // LANES, pieces * n_slots * (span + 8), LANES), jnp.float32),
            pltpu.VMEM((pieces, n_slots, span, width), jnp.bfloat16),
            pltpu.VMEM((16, LANES) if rims else (UP * seg, width), jnp.bfloat16),
            pltpu.SMEM((n_slots + 1,), jnp.int32),
            pltpu.SMEM((n_slots + 1,), jnp.int32),
            pltpu.SMEM((17,), jnp.int32),
            pltpu.SemaphoreType.DMA((width // STEP + 1, 2 * UP)),
            pltpu.SemaphoreType.DMA((pieces, n_slots)),
            pltpu.SemaphoreType.DMA((n_slots,)),
        ],
        compiler_params=pltpu.CompilerParams(vmem_limit_bytes=58 * 2**20),
        cost_estimate=pl.CostEstimate(
            flops=2 * 48 * pieces * frames * 2 * channels * UP * width,
            bytes_accessed=2 * (w_up.size + w_pre.size + 48 * pieces * span * width),
            transcendentals=0,
        ),
        name="edges" if rims else "inner",
    )(*operands)


def one_hot_rows(match, values):
    rows = jnp.dot(match.astype(jnp.bfloat16), values.reshape(values.shape[0], -1), preferred_element_type=jnp.float32)
    return rows.astype(jnp.bfloat16)


def packed(features, target):
    n_slots, seg, feat = features.shape
    used = target >= 0
    worker = jnp.where(used, target // 32, -1)
    order = jnp.arange(n_slots, dtype=jnp.int32)
    rank = jnp.sum(((worker[:, None] == worker[None, :]) & (order[:, None] < order[None, :])).astype(jnp.int32), axis=0)
    slot = target % 32 + 1

    def sorted_rows(worker_of, values):
        row = jnp.where(used, worker_of * CAP + rank, -1)
        select = row[None, :] == jnp.arange(16 * CAP, dtype=jnp.int32)[:, None]
        code = jnp.sum(jnp.where(select, slot[None, :], 0), axis=1).astype(jnp.bfloat16)
        return one_hot_rows(select, values).reshape(16, CAP, RIM, feat), code.reshape(16, CAP)

    heads, head_code = sorted_rows(worker, features[:, :RIM])
    tails, tail_code = sorted_rows((worker + 1) % 16, features[:, seg - RIM :])
    codes = jnp.concatenate([tail_code, head_code], axis=1)
    codes = jnp.broadcast_to(codes[:, None, :, None], (16, 1, 2 * CAP, feat))
    return jnp.concatenate([jnp.concatenate([tails, heads], axis=2), codes], axis=1)


def swapped(got):
    def codes(first):
        return got[:, CAP, first : first + CAP, 0].astype(jnp.int32).reshape(-1)

    def entries(first):
        return got[:, :CAP, first : first + RIM].reshape(got.shape[0] * CAP, -1)

    tail_code, head_code = codes(0), codes(RIM)
    match = (tail_code[:, None] == head_code[None, :]) & (tail_code[:, None] > 0)
    shape = (got.shape[0], CAP, RIM, got.shape[3])
    heads = one_hot_rows(match, entries(RIM)).reshape(shape)
    tails = one_hot_rows(match.T, entries(0)).reshape(shape)
    return jnp.concatenate([heads, tails], axis=2)


def from_groups(own):
    gen, count = lax.axis_index("gen"), lax.axis_size("gen")
    lower = lax.ppermute(own, "gen", [(g, (g + 1) % count) for g in range(count)])[:, :RIM]
    upper = lax.ppermute(own, "gen", [(g, (g - 1) % count) for g in range(count)])[:, RIM:]
    tail_code, head_code = lower[CAP].astype(jnp.float32), upper[CAP].astype(jnp.float32)
    stepped = jnp.where(tail_code == 32, 1.0, tail_code + 1)
    tail_code = jnp.where((gen == 0) & (tail_code > 0), stepped, tail_code)
    stepped = jnp.where(head_code == 1, 32.0, head_code - 1)
    head_code = jnp.where((gen == count - 1) & (head_code > 0), stepped, head_code)
    codes = jnp.concatenate([tail_code, head_code], axis=0).astype(own.dtype)
    return jnp.concatenate([jnp.concatenate([lower[:CAP], upper[:CAP]], axis=1), codes[None]], axis=0)


def on_device(features, target, extents, w_pre, biases, snake_params, w_up, up_bias):
    rims = packed(features, target)
    plan = jnp.concatenate([target, extents.reshape(-1)])
    far = from_groups(lax.optimization_barrier((rims[0], plan))[0])
    got = lax.all_to_all(rims, "voc", split_axis=0, concat_axis=0, tiled=True)
    back = jnp.concatenate([swapped(got), jnp.broadcast_to(far, rims.shape)], axis=1)
    home = lax.all_to_all(back, "voc", split_axis=0, concat_axis=0, tiled=True)
    vectors = jnp.concatenate([biases, snake_params.reshape(-1), up_bias])[None, :]
    rest = (plan, features, w_pre, w_up, vectors)
    waves = vocode((RIM,), 16, None, None, *rest)
    return vocode((0, 20), 4, home, waves, *rest)


def solution(mesh):
    split = P(("gen", "voc"))
    return jax.shard_map(
        on_device,
        mesh=mesh,
        in_specs=(split, split, split, P(), P(), P(), P(), P()),
        out_specs=split,
        check_vma=False,
    )
```

```python
import functools

import jax
import jax.numpy as jnp
from jax import lax
from jax.experimental import pallas as pl
from jax.experimental.pallas import tpu as pltpu
from jax.sharding import PartitionSpec as P

UP = 4
KPRE = 7
RIM = 4
CAP = 4
LANES = 128
STEP = 256

SIN2 = (9.869604311707747, -32.46967117172015, 42.72719633651888, -30.101465841328583, 13.050098920339147, -3.3565926218240247)


def copy_of(src, dst, sem):
    return pltpu.make_async_copy(src, dst, sem)


def vocode_kernel(starts, frames, rims, plan, features, *rest):
    if rims:
        home, w_pre, w_up, vectors, _, out = rest[:6]
        scratch = rest[6:]
    else:
        home = None
        w_pre, w_up, vectors, out = rest[:4]
        scratch = rest[4:]
    (wp, wu, win, msk, taps, acts, rows32, stage, zeros, slots, ranks, counts, w_sem, out_sem, zero_sem) = scratch
    pieces = len(starts)
    act_rows = frames + 2
    win_rows = frames + 8
    seg = features.shape[1]
    channels = wp.shape[1]
    width = wu.shape[1] // (2 * UP)
    n_slots = features.shape[0]
    span = UP * frames
    pitch = span + 8
    parts = width // STEP
    tiles = STEP // LANES

    phases = tuple((r + UP // 2, r + UP + UP // 2 if r < UP // 2 else r - UP // 2) for r in range(UP))

    def load_taps(n, start):
        for tap in sum(phases, ()):
            cols = pl.ds(pl.multiple_of(tap * width + n * STEP, STEP), STEP)
            copy = copy_of(w_up.at[:, cols], wu.at[:, cols], w_sem.at[n, tap])
            copy.start() if start else copy.wait()

    def load_pre(start):
        copy = copy_of(w_pre, wp, w_sem.at[parts, 0])
        copy.start() if start else copy.wait()

    load_pre(True)
    for n in range(parts):
        load_taps(n, True)
    for v in range(17):
        counts[v] = 0
    slots[0] = 0
    ranks[0] = 0

    def scan(i, found):
        code = plan[i]
        used = code >= 0
        slots[found] = i
        if rims:
            worker = jnp.where(used, lax.shift_right_logical(code, 5), 16)
            rank = counts[worker]
            ranks[found] = rank
            counts[worker] = rank + 1
        return found + used.astype(jnp.int32)

    found = lax.fori_loop(0, n_slots, scan, jnp.int32(0), unroll=8)

    cell = lax.broadcasted_iota(jnp.int32, (seg, LANES), 0)
    rim_cell = lax.broadcasted_iota(jnp.int32, (2 * RIM, LANES), 0)

    def fill(block, b):
        c = jnp.minimum(b, found - 1)
        slot = slots[c]
        own = (cell < plan[n_slots + slot * 3]).astype(jnp.float32)
        values = features[slot].astype(jnp.float32) * own
        if not rims:
            win[0, pl.ds(b, seg, stride=block), :] = values
            msk[0, pl.ds(b, seg, stride=block), :] = own
        else:
            at = RIM * block + b
            inner = win_rows - RIM
            win[0, pl.ds(at, inner, stride=block), :] = values[:inner]
            msk[0, pl.ds(at, inner, stride=block), :] = own[:inner]
            win[1, pl.ds(b, inner, stride=block), :] = values[seg - inner :]
            msk[1, pl.ds(b, inner, stride=block), :] = own[seg - inner :]
            worker = lax.shift_right_logical(plan[slot], 5)
            rank = ranks[c]
            before_ok = (rim_cell - RIM + seg - RIM < plan[n_slots + slot * 3 + 1]).astype(jnp.float32)
            after_ok = (rim_cell < plan[n_slots + slot * 3 + 2]).astype(jnp.float32)
            before = home[worker, rank].astype(jnp.float32) * before_ok
            after = home[(worker + 1) & 15, rank].astype(jnp.float32) * after_ok
            win[0, pl.ds(b, RIM, stride=block), :] = before[RIM:]
            msk[0, pl.ds(b, RIM, stride=block), :] = before_ok[RIM:]
            tail = inner * block + b
            win[1, pl.ds(tail, RIM, stride=block), :] = after[:RIM]
            msk[1, pl.ds(tail, RIM, stride=block), :] = after_ok[:RIM]

            def far(row, rows_from):
                code = (plan[slot] & 31).astype(jnp.float32) + 1.0

                def look(k, total):
                    codes = home[k, 2 * CAP].astype(jnp.float32)
                    for e in range(CAP):
                        entry = home[k, CAP + e].astype(jnp.float32)
                        total = total + jnp.where(codes[row + e : row + e + 1] == code, entry, 0.0)
                    return total

                total = lax.fori_loop(0, home.shape[0], look, jnp.zeros((2 * RIM, LANES), jnp.float32), unroll=8)
                return total[rows_from : rows_from + RIM]

            @pl.when(worker == 0)
            def _():
                win[0, pl.ds(b, RIM, stride=block), :] = far(0, 0) * before_ok[RIM:]

            @pl.when(worker == 15)
            def _():
                win[1, pl.ds(tail, RIM, stride=block), :] = far(CAP, RIM) * after_ok[:RIM]

    def run(block):
        rows = act_rows * block

        def fill_one(b, c):
            fill(block, b)
            return c

        lax.fori_loop(0, block, fill_one, 0, unroll=2)
        for p in range(pieces):
            for q in range(KPRE):
                taps[pl.ds(p * rows, rows), pl.ds(q * LANES, LANES)] = win[p, pl.ds(q * block, rows), :].astype(
                    jnp.bfloat16
                )

        load_pre(False)

        if not rims:
            zeros[...] = jnp.zeros_like(zeros)

            def clear(i, c):
                @pl.when(plan[i] < 0)
                def _():
                    copy_of(zeros, out.at[i], zero_sem.at[i]).start()

                return c

            lax.fori_loop(0, n_slots, clear, 0)

        def conv_chunk(n, c):
            def vector(i):
                return vectors[:, pl.ds(pl.multiple_of(i * channels + n * STEP, STEP), STEP)]

            cols = pl.ds(pl.multiple_of(n * STEP, STEP), STEP)
            bias = vector(0)
            scale = vector(1) * (1.0 / jnp.pi)
            inverse = 1.0 / vector(2)
            for p in range(pieces):
                sums = jnp.dot(taps[pl.ds(p * rows, rows), :], wp[:, cols], preferred_element_type=jnp.float32)
                mask = msk[p, pl.ds(3 * block, rows), :]
                hidden = jnp.concatenate([mask] * tiles, axis=1) * (sums + bias)
                turns = hidden * scale
                rest_of = turns - jnp.floor(turns + 0.5)
                u = rest_of * rest_of
                poly = SIN2[-1] * u + SIN2[-2]
                for coef in SIN2[-3::-1]:
                    poly = poly * u + coef
                acts[pl.ds(p * rows, rows), cols] = (hidden + u * poly * inverse).astype(jnp.bfloat16)
            return c

        lax.fori_loop(0, channels // STEP, conv_chunk, 0, unroll=2)

        def acts_from(shift):
            picked = [acts[pl.ds(p * rows + shift * block, frames * block), :] for p in range(pieces)]
            return picked[0] if pieces == 1 else jnp.concatenate(picked, axis=0)

        def up_part(n, c):
            load_taps(n, False)
            for r in range(UP):
                sums = vectors[:, pl.ds(pl.multiple_of(3 * channels + n * STEP, STEP), STEP)]
                for tap, shift in zip(phases[r], (1, 0 if r < UP // 2 else 2)):
                    cols = pl.ds(pl.multiple_of(tap * width + n * STEP, STEP), STEP)
                    sums = sums + jnp.dot(acts_from(shift), wu[:, cols], preferred_element_type=jnp.float32)
                for p in range(pieces):
                    for j in range(frames):
                        mask = msk[p, pl.ds((j + 4) * block, block), :]
                        here = (p * frames + j) * block
                        for half in range(tiles):
                            rows32[
                                n * tiles + half, pl.ds(p * block * pitch + UP * j + r, block, stride=pitch), :
                            ] = mask * sums[here : here + block, half * LANES : (half + 1) * LANES]
            return c

        lax.fori_loop(0, parts, up_part, 0)

        def send(b, c):
            for p in range(pieces):
                for n in range(width // LANES):
                    stage[p, b, :, n * LANES : (n + 1) * LANES] = rows32[
                        n, pl.ds(pl.multiple_of((p * block + b) * pitch, 8), span), :
                    ].astype(jnp.bfloat16)

            @pl.when(b < found)
            def _():
                for p in range(pieces):
                    copy_of(stage.at[p, b], out.at[slots[b], pl.ds(UP * starts[p], span)], out_sem.at[p, b]).start()

            return c

        lax.fori_loop(0, block, send, 0)

    for units in range(1, 5):

        @pl.when((found > 16 * (units - 1)) & (found <= 16 * units))
        def _(units=units):
            run(16 * units)

    @pl.when(found == 0)
    def _():
        load_pre(False)
        for n in range(parts):
            load_taps(n, False)
        if not rims:
            zeros[...] = jnp.zeros_like(zeros)

            def clear(i, c):
                copy_of(zeros, out.at[i], zero_sem.at[i]).start()
                return c

            lax.fori_loop(0, n_slots, clear, 0)

    def settle(b, c):
        for p in range(pieces):
            copy_of(stage.at[p, b], out.at[0, pl.ds(0, span)], out_sem.at[p, b]).wait()
        return c

    lax.fori_loop(0, found, settle, 0)

    if not rims:

        def cleared(i, c):
            @pl.when(plan[i] < 0)
            def _():
                copy_of(zeros, out.at[i], zero_sem.at[i]).wait()

            return c

        lax.fori_loop(0, n_slots, cleared, 0)


def vocode(starts, frames, home, waves, plan, features, w_pre, w_up, vectors):
    rims = home is not None
    pieces = len(starts)
    n_slots, seg, feat = features.shape
    channels = w_pre.shape[1]
    width = w_up.shape[1] // (2 * UP)
    span = UP * frames
    smem = pl.BlockSpec(memory_space=pltpu.SMEM)
    vmem = pl.BlockSpec(memory_space=pltpu.VMEM)
    hbm = pl.BlockSpec(memory_space=pl.ANY)
    operands = [plan, features]
    specs = [smem, vmem]
    if rims:
        operands.append(home)
        specs.append(vmem)
    operands += [w_pre, w_up, vectors]
    specs += [hbm, hbm, vmem]
    aliases = {}
    if rims:
        aliases = {len(operands): 0}
        operands.append(waves)
        specs.append(hbm)
    return pl.pallas_call(
        functools.partial(vocode_kernel, starts, frames, rims),
        out_shape=jax.ShapeDtypeStruct((n_slots, UP * seg, width), jnp.bfloat16),
        in_specs=specs,
        out_specs=hbm,
        input_output_aliases=aliases,
        scratch_shapes=[
            pltpu.VMEM(w_pre.shape, jnp.bfloat16),
            pltpu.VMEM(w_up.shape, jnp.bfloat16),
            pltpu.VMEM((pieces, (frames + 8) * n_slots, feat), jnp.float32),
            pltpu.VMEM((pieces, (frames + 8) * n_slots, feat), jnp.float32),
            pltpu.VMEM((pieces * (frames + 2) * n_slots, KPRE * feat), jnp.bfloat16),
            pltpu.VMEM((pieces * (frames + 2) * n_slots, channels), jnp.bfloat16),
            pltpu.VMEM((width // LANES, pieces * n_slots * (span + 8), LANES), jnp.float32),
            pltpu.VMEM((pieces, n_slots, span, width), jnp.bfloat16),
            pltpu.VMEM((16, LANES) if rims else (UP * seg, width), jnp.bfloat16),
            pltpu.SMEM((n_slots + 1,), jnp.int32),
            pltpu.SMEM((n_slots + 1,), jnp.int32),
            pltpu.SMEM((17,), jnp.int32),
            pltpu.SemaphoreType.DMA((width // STEP + 1, 2 * UP)),
            pltpu.SemaphoreType.DMA((pieces, n_slots)),
            pltpu.SemaphoreType.DMA((n_slots,)),
        ],
        compiler_params=pltpu.CompilerParams(vmem_limit_bytes=58 * 2**20),
        cost_estimate=pl.CostEstimate(
            flops=2 * 48 * pieces * frames * 2 * channels * UP * width,
            bytes_accessed=2 * (w_up.size + w_pre.size + 48 * pieces * span * width),
            transcendentals=0,
        ),
        name="edges" if rims else "inner",
    )(*operands)


def one_hot_rows(match, values):
    rows = jnp.dot(match.astype(jnp.bfloat16), values.reshape(values.shape[0], -1), preferred_element_type=jnp.float32)
    return rows.astype(jnp.bfloat16)


def packed(features, target):
    n_slots, seg, feat = features.shape
    used = target >= 0
    worker = jnp.where(used, target // 32, -1)
    order = jnp.arange(n_slots, dtype=jnp.int32)
    rank = jnp.sum(((worker[:, None] == worker[None, :]) & (order[:, None] < order[None, :])).astype(jnp.int32), axis=0)
    slot = target % 32 + 1

    def sorted_rows(worker_of, values):
        row = jnp.where(used, worker_of * CAP + rank, -1)
        select = row[None, :] == jnp.arange(16 * CAP, dtype=jnp.int32)[:, None]
        code = jnp.sum(jnp.where(select, slot[None, :], 0), axis=1).astype(jnp.bfloat16)
        return one_hot_rows(select, values).reshape(16, CAP, RIM, feat), code.reshape(16, CAP)

    heads, head_code = sorted_rows(worker, features[:, :RIM])
    tails, tail_code = sorted_rows((worker + 1) % 16, features[:, seg - RIM :])
    codes = jnp.concatenate([tail_code, head_code], axis=1)
    codes = jnp.broadcast_to(codes[:, None, :, None], (16, 1, 2 * CAP, feat))
    return jnp.concatenate([jnp.concatenate([tails, heads], axis=2), codes], axis=1)


def swapped(got):
    def codes(first):
        return got[:, CAP, first : first + CAP, 0].astype(jnp.int32).reshape(-1)

    def entries(first):
        return got[:, :CAP, first : first + RIM].reshape(got.shape[0] * CAP, -1)

    tail_code, head_code = codes(0), codes(RIM)
    match = (tail_code[:, None] == head_code[None, :]) & (tail_code[:, None] > 0)
    shape = (got.shape[0], CAP, RIM, got.shape[3])
    heads = one_hot_rows(match, entries(RIM)).reshape(shape)
    tails = one_hot_rows(match.T, entries(0)).reshape(shape)
    return jnp.concatenate([heads, tails], axis=2)


def from_groups(own):
    gen, count = lax.axis_index("gen"), lax.axis_size("gen")
    lower = lax.ppermute(own, "gen", [(g, (g + 1) % count) for g in range(count)])[:, :RIM]
    upper = lax.ppermute(own, "gen", [(g, (g - 1) % count) for g in range(count)])[:, RIM:]
    tail_code, head_code = lower[CAP].astype(jnp.float32), upper[CAP].astype(jnp.float32)
    stepped = jnp.where(tail_code == 32, 1.0, tail_code + 1)
    tail_code = jnp.where((gen == 0) & (tail_code > 0), stepped, tail_code)
    stepped = jnp.where(head_code == 1, 32.0, head_code - 1)
    head_code = jnp.where((gen == count - 1) & (head_code > 0), stepped, head_code)
    codes = jnp.concatenate([tail_code, head_code], axis=0).astype(own.dtype)
    return jnp.concatenate([jnp.concatenate([lower[:CAP], upper[:CAP]], axis=1), codes[None]], axis=0)


def on_device(features, target, extents, w_pre, biases, snake_params, w_up, up_bias):
    rims = packed(features, target)
    plan = jnp.concatenate([target, extents.reshape(-1)])
    far = from_groups(lax.optimization_barrier((rims[0], plan))[0])
    got = lax.all_to_all(rims, "voc", split_axis=0, concat_axis=0, tiled=True)
    back = jnp.concatenate([swapped(got), jnp.broadcast_to(far, rims.shape)], axis=1)
    home = lax.all_to_all(back, "voc", split_axis=0, concat_axis=0, tiled=True)
    vectors = jnp.concatenate([biases, snake_params.reshape(-1), up_bias])[None, :]
    rest = (plan, features, w_pre, w_up, vectors)
    waves = vocode((RIM,), 16, None, None, *rest)
    return vocode((0, 20), 4, home, waves, *rest)


def solution(mesh):
    split = P(("gen", "voc"))
    return jax.shard_map(
        on_device,
        mesh=mesh,
        in_specs=(split, split, split, P(), P(), P(), P(), P()),
        out_specs=split,
        check_vma=False,
    )
```
